32 devices in a mesh: mem: 4 (over x, core), lev: 8 (over z, y).
Axes of the slice: x: 2, y: 2, z: 4, core: 2. Of those that a mesh axis runs over, the one named last changes fastest.
Arguments:
- control: float32 [4, 128, 128, 256], P('mem', 'lev'), may hold values from -6 to 6
- diffusivity: float32 [128, 128, 256], P('lev'), may hold values from 0.02 to 0.24
- perturb: float32 [4, 49152, 128], P('mem', 'lev'), may hold values from -6 to 6
- vertical_filter: float32 [128, 128], replicated, may hold values from -0.5 to 0.5
- sub_widths: int32 [8], replicated, may hold values from 1 to 6144, 32768 in all
- obs_raw: int32 [8, 6144], P('lev'), may hold values from 0 to 1048575
- obs_counts: int32 [8], replicated, may hold values from 1 to 6144, 43008 in all
- obs_rinv: float32 [8, 6144, 128], P('lev'), may hold values from 0.3 to 3
Outputs:
- ensemble_term: float32 [4, 128, 128, 256], P('mem', 'lev')
The draws below stay inside these ranges and needn't reach their ends.
Inputs may be any that keep to these rules, and one draw needn't show every extreme that they name: `sub_widths`: the widths sum to 32768; the largest is exactly 6144. `obs_counts`: the counts sum to 43008; the largest is exactly 6144.
All inputs are finite; a program needn't handle non-finite values.
Results may differ from the reference program's by a relative error of at most 0.00011.
Values sent between devices are 32-bit elements; how exact they have to be, the bound alone decides.
No kernel may reach another device: no remote copies, remote signals or barrier semaphores. Data moves between devices by JAX's collectives and lax.ppermute only.
A program may use at most 192 MiB of HBM per device.

```python
import math
import jax
import jax.numpy as jnp
import numpy as np
from jax import lax

NX = 128
NY = 256
STEPS = 4
MEM = 4
LEVELS = 128
SUB_CAP = 6144
OBS_CAP = 6144
N_LEV = 8


def plant(entries, key, least, largest):
    longest = entries.shape.index(max(entries.shape))
    spots = []
    for shift in (0, 1):
        where = [jax.random.randint(jax.random.fold_in(key, axis), (), 0, length) for axis, length in enumerate(entries.shape)]
        where[longest] = (where[longest] + shift) % entries.shape[longest]
        spots.append(tuple(where))
    return entries.at[spots[0]].set(least).at[spots[1]].set(largest)


def shard_levels(own_key, shape, split, least, high):
    loudness = 1.0
    for dim, shards_of in split:
        heights = jax.random.uniform(jax.random.fold_in(jax.random.fold_in(own_key, 6), dim), (shards_of,), jnp.float32, least / len(split), high / len(split))
        loudness = loudness * jnp.repeat(jnp.exp(heights), shape[dim] // shards_of).reshape((-1,) + (1,) * (len(shape) - 1 - dim))
    return loudness


def length_profile(amount, total, limit, lean):
    weights = [(1 << 20) // math.isqrt(rank ** lean) + 1 for rank in range(2, amount + 1)]
    spare, holding = total - limit - (amount - 1), [1] * (amount - 1)
    while spare > 0:
        candidates = [i for i in range(amount - 1) if holding[i] < limit]
        pool, remaining = sum([weights[i] for i in candidates]), spare
        for i in candidates:
            more = min(limit - holding[i], max(1, remaining * weights[i] // pool), spare)
            holding[i] = holding[i] + more
            spare = spare - more
    return np.array([limit] + holding)


def uneven(stream_key, amount, total, limit, skew):
    if amount == 2:
        one = jax.random.randint(stream_key, (), max(1, total - limit), min(limit, total - 1) + 1)
        return jnp.stack([one, total - one])
    lengths = jnp.asarray(length_profile(amount, total, limit, skew), jnp.int32)
    pairs = (amount - 1) // 2
    giver, sink = lengths[1:1 + 2 * pairs:2], lengths[2:2 + 2 * pairs:2]
    room = jnp.minimum(giver - 1, limit - sink)
    moved = jax.random.randint(jax.random.fold_in(stream_key, 1), (pairs,), 0, 1 << 20) % (room + 1)
    lengths = lengths.at[1:1 + 2 * pairs:2].set(giver - moved).at[2:2 + 2 * pairs:2].set(sink + moved)
    return lengths[jax.random.permutation(jax.random.fold_in(stream_key, 2), amount)]


def bell_draw(key, dims, spread, most, split=(), held_as=jnp.bfloat16):
    drawn = jax.random.normal(key, dims, jnp.float32) * spread
    if len(split) > 0:
        drawn = shard_levels(key, dims, split, -0.22, 0.18) * drawn
    return jnp.clip(drawn, min=-most, max=most).astype(held_as)


def setup_inputs(seed: int = 0) -> dict:
    seeds = jax.random.split(jax.random.key(seed), 9)
    return {
        "control": bell_draw(seeds[0], (MEM, LEVELS, NX, NY), 1.0, 6.0, ((0, 4), (1, 8)), jnp.float32),
        "diffusivity": jnp.clip(jnp.exp(math.log(0.24) - 2.4849066 * jax.random.uniform(seeds[1], (LEVELS, NX, NY), jnp.float32) ** shard_levels(seeds[1], (LEVELS, NX, NY), ((0, 8),), -0.2, 0.2)), 0.02, 0.24),
        "perturb": bell_draw(seeds[2], (MEM, N_LEV * SUB_CAP, LEVELS), (MEM ** -0.25), 6.0, ((0, 4), (1, 8)), jnp.float32),
        "vertical_filter": bell_draw(seeds[3], (LEVELS, LEVELS), LEVELS ** -0.5, 0.5, (), jnp.float32),
        "sub_widths": uneven(seeds[4], N_LEV, NX * NY, SUB_CAP, 2).astype(jnp.int32),
        "obs_raw": plant(jax.random.randint(seeds[5], (N_LEV, OBS_CAP), 0, 1048576), jax.random.fold_in(seeds[5], 1), 0, 1048575).astype(jnp.int32),
        "obs_counts": uneven(seeds[6], N_LEV, N_LEV * OBS_CAP * 7 // 8, OBS_CAP, 2).astype(jnp.int32),
        "obs_rinv": jnp.clip(jnp.exp(math.log(3.0) - 2.3025851 * jax.random.uniform(seeds[7], (N_LEV, OBS_CAP, LEVELS), jnp.float32) ** shard_levels(seeds[7], (N_LEV, OBS_CAP, LEVELS), ((0, 8),), -0.2, 0.2)), 0.3, 3.0),
    }


def diffuse(values, diffusivity):
    face_x = 0.5 * (diffusivity[..., 1:, :] + diffusivity[..., :-1, :])
    face_y = 0.5 * (diffusivity[..., :, 1:] + diffusivity[..., :, :-1])
    leading = [(0, 0)] * (values.ndim - 2)
    for repeat in range(STEPS):
        flux_x = face_x * (values[..., 1:, :] - values[..., :-1, :])
        flux_y = face_y * (values[..., :, 1:] - values[..., :, :-1])
        padded_x = jnp.pad(flux_x, leading + [(1, 1), (0, 0)])
        padded_y = jnp.pad(flux_y, leading + [(0, 0), (1, 1)])
        values = values + (padded_x[..., 1:, :] - padded_x[..., :-1, :]) + (padded_y[..., :, 1:] - padded_y[..., :, :-1])
    return values


def row_tables(sub_widths, capacity, columns):
    widths = sub_widths.astype(jnp.int32)
    starts = (jnp.cumsum(widths) - widths).astype(jnp.int32)
    rows_all = jnp.arange(widths.shape[0] * capacity, dtype=jnp.int32)
    owner = (rows_all // capacity).astype(jnp.int32)
    offset = (rows_all % capacity).astype(jnp.int32)
    valid = offset < widths[owner]
    target = jnp.where(valid, starts[owner] + offset, columns).astype(jnp.int32)
    source = jnp.minimum(target, columns - 1).astype(jnp.int32)
    return target, source


def reference(control, diffusivity, perturb, vertical_filter, sub_widths, obs_raw, obs_counts, obs_rinv):
    columns = NX * NY
    highest = lax.Precision.HIGHEST
    target, source = row_tables(sub_widths, SUB_CAP, columns)

    def accumulate(total, member):
        member_control, member_perturb = member
        smooth = diffuse(member_control, diffusivity).reshape(LEVELS, columns)
        column_form = jnp.take(smooth, source, axis=1).T
        filtered = jnp.dot(column_form, vertical_filter.T, precision=highest)
        return total + member_perturb * filtered, None

    increment, unused = lax.scan(accumulate, jnp.zeros((N_LEV * SUB_CAP, LEVELS), jnp.float32), (control, perturb))
    widths = sub_widths.astype(jnp.int32)
    slots = (obs_raw.astype(jnp.int32) % widths[:, None]).astype(jnp.int32)
    obs_rows = (jnp.arange(N_LEV, dtype=jnp.int32)[:, None] * SUB_CAP + slots).astype(jnp.int32)
    live = jnp.arange(OBS_CAP, dtype=jnp.int32)[None, :] < obs_counts.astype(jnp.int32)[:, None]
    weighted = jnp.where(live[..., None], obs_rinv * increment[obs_rows], jnp.zeros_like(obs_rinv))
    adjoint_obs = jnp.zeros_like(increment).at[obs_rows.reshape(-1)].add(weighted.reshape(-1, LEVELS))

    def backward(member_perturb):
        back_filtered = jnp.dot(member_perturb * adjoint_obs, vertical_filter, precision=highest)
        grid = jnp.zeros((columns + 1, LEVELS), jnp.float32).at[target].add(back_filtered)[:columns]
        return diffuse(grid.T.reshape(LEVELS, NX, NY), diffusivity)

    return lax.map(backward, perturb)
```

```python
import functools

import jax
import jax.numpy as jnp
from jax import lax
from jax.experimental import pallas as pl
from jax.experimental.pallas import tpu as pltpu
from jax.sharding import PartitionSpec as P

STEPS = 4
PARTS = 3
LANES = 128
GROUP = 8
F32 = jnp.float32
BF16 = jnp.bfloat16


def flip_pairs(size, bit):
    return [(i, i ^ bit) for i in range(size)]


def transpose_in(src, dst, size_x):
    def step(b, _):
        first = pl.multiple_of(b * 8, 8)
        dst[pl.ds(first, 8)] = jnp.swapaxes(src[:, pl.ds(first, 8), :], 0, 1)
        return 0

    lax.fori_loop(0, size_x // 8, step, 0, unroll=2)


def faces(diff, kx, ky, size_x, size_y):
    lane = lax.broadcasted_iota(jnp.int32, (GROUP, size_y), 1)

    def step(x, here):
        following = diff[jnp.minimum(x + 1, size_x - 1)]
        kx[x] = jnp.where(x < size_x - 1, 0.5 * (here + following), 0.0)
        ahead = pltpu.roll(here, size_y - 1, 1)
        ky[x] = jnp.where(lane < size_y - 1, 0.5 * (here + ahead), 0.0)
        return following

    lax.fori_loop(0, size_x, step, diff[0], unroll=4)


def sweep(read, write, kx, ky, size_x, size_y):
    def step(x, carry):
        here, flux_before = carry
        following = read(jnp.minimum(x + 1, size_x - 1))
        flux_x = kx[x] * (following - here)
        flux_y = ky[x] * (pltpu.roll(here, size_y - 1, 1) - here)
        write(x, here + (flux_x - flux_before) + (flux_y - pltpu.roll(flux_y, 1, 1)))
        return following, flux_x

    first = read(0)
    lax.fori_loop(0, size_x, step, (first, jnp.zeros_like(first)), unroll=8)


def forward_kernel(size_x, size_y, groups, capacity, starts, info, control, diffusivity, diff_out, *rest):
    outs = rest[: groups * PARTS]
    grid, flat, kx, ky = rest[groups * PARTS :]
    columns = size_x * size_y
    part = capacity // PARTS
    transpose_in(diffusivity, diff_out, size_x)
    faces(diff_out, kx, ky, size_x, size_y)
    transpose_in(control.at[0], grid, size_x)

    def read(x):
        return grid[x]

    def write(x, value):
        grid[x] = value

    def write_flat(x, value):
        flat[:, pl.ds(pl.multiple_of(x * size_y, size_y), size_y)] = value

    for repeat in range(STEPS - 1):
        sweep(read, write, kx, ky, size_x, size_y)
    sweep(read, write_flat, kx, ky, size_x, size_y)
    flat[:, columns:] = jnp.zeros((GROUP, flat.shape[1] - columns), F32)

    lane = lax.broadcasted_iota(jnp.int32, (GROUP, LANES), 1)
    me = info[0]
    tiles = part // LANES
    for d in range(groups):
        start = starts[jnp.bitwise_xor(me, d)]
        base = start // LANES
        shift = start - base * LANES
        back = lax.rem(LANES - shift, LANES)
        low = lane < LANES - shift
        for c in range(PARTS):
            out = outs[c * groups + d]
            begin = base + c * tiles

            def load(t):
                at = pl.multiple_of((begin + t) * LANES, LANES)
                return pltpu.roll(flat[:, pl.ds(at, LANES)], back, 1)

            now = load(0)
            for t in range(tiles):
                later = load(t + 1)
                out[:, t * LANES : (t + 1) * LANES] = jnp.where(low, now, later)
                now = later


def split3(value):
    high = value.astype(BF16)
    return high, (value - high.astype(F32)).astype(BF16)


def dot3(a, b, dims):
    ah, al = split3(a)
    bh, bl = split3(b)
    dot = functools.partial(lax.dot_general, dimension_numbers=(dims, ((), ())), preferred_element_type=F32)
    return dot(ah, bh) + (dot(ah, bl) + dot(al, bh))


def observation_kernel(rows_here, obs_cap, info, slots, rinv, out, split):
    step = pl.program_id(0)

    @pl.when(step == 0)
    def _():
        values = rinv[0]
        high = values.astype(BF16)
        split[:, :LANES] = high
        split[:, LANES:] = (values - high.astype(F32)).astype(BF16)

    first = info[2] + step * rows_here
    block = 512
    row = first + lax.broadcasted_iota(jnp.int32, (rows_here, block), 0)

    def add(b, total):
        at = pl.multiple_of(b * block, block)
        hit = row == slots[:, pl.ds(at, block)]
        onehot = jnp.where(hit, 1.0, 0.0).astype(BF16)
        return total + jnp.dot(onehot, split[pl.ds(at, block), :], preferred_element_type=F32)

    total = lax.fori_loop(0, obs_cap // block, add, jnp.zeros((rows_here, 2 * LANES), F32))
    out[...] = total[:, :LANES] + total[:, LANES:]


def filter_kernel(groups, info, vfilter, perturb, *rest):
    pieces = rest[:groups]
    keep, send = rest[groups:]
    half = keep.shape[0]
    width = 256
    mine = info[1]
    for which, out in ((mine, keep), (1 - mine, send)):

        def step(b, _):
            at = pl.multiple_of(which * half + b * width, width)
            slab = jnp.concatenate([piece[:, pl.ds(at, width)] for piece in pieces], axis=0)
            filtered = dot3(slab.T, vfilter[...], ((1,), (1,)))
            out[pl.ds(pl.multiple_of(b * width, width), width), :] = (
                perturb[0, pl.ds(at, width), :] * filtered
            )
            return 0

        lax.fori_loop(0, half // width, step, 0, unroll=2)


def back_kernel(groups, info, vfilter, perturb, adj_mine, adj_other, *pieces):
    half = adj_mine.shape[0]
    width = 256
    levels = pieces[0].shape[0]
    mine = info[1]
    for which, adj in ((mine, adj_mine), (1 - mine, adj_other)):

        def step(b, _):
            at = pl.multiple_of(which * half + b * width, width)
            weighted = perturb[0, pl.ds(at, width), :] * adj[pl.ds(pl.multiple_of(b * width, width), width), :]
            result = dot3(vfilter[...], weighted, ((0,), (1,)))
            for d in range(groups):
                pieces[d][:, pl.ds(at, width)] = result[d * levels : (d + 1) * levels]
            return 0

        lax.fori_loop(0, half // width, step, 0, unroll=2)


def backward_kernel(size_x, size_y, groups, capacity, starts, info, diff, *rest):
    ins = rest[: groups * PARTS]
    out, staging, flat, grid, kx, ky, sem = rest[groups * PARTS :]
    part = capacity // PARTS
    me = info[0]
    step_id = pl.program_id(0)
    level = pl.multiple_of(step_id * GROUP, GROUP)
    copies = []
    for c in range(PARTS):
        for d in range(groups):
            copies.append(
                pltpu.make_async_copy(
                    ins[c * groups + d].at[pl.ds(level, GROUP), :],
                    staging.at[jnp.bitwise_xor(me, d), :, pl.ds(c * part, part)],
                    sem.at[c * groups + d],
                )
            )
    for copy in copies:
        copy.start()
    faces(diff, kx, ky, size_x, size_y)
    for copy in copies:
        copy.wait()

    lane = lax.broadcasted_iota(jnp.int32, (GROUP, LANES), 1)
    tiles = capacity // LANES
    some = 8

    def place(j, _):
        start = starts[j]
        base = start // LANES
        shift = start - base * LANES
        high = lane >= shift

        def several(b, before):
            for t in range(some):
                at = pl.multiple_of((b * some + t) * LANES, LANES)
                to = pl.multiple_of((base + b * some + t) * LANES, LANES)
                here = pltpu.roll(staging[j, :, pl.ds(at, LANES)], shift, 1)
                flat[:, pl.ds(to, LANES)] = jnp.where(high, here, before)
                before = here
            return before

        existing = flat[:, pl.ds(pl.multiple_of(base * LANES, LANES), LANES)]
        last = lax.fori_loop(0, tiles // some, several, existing)
        flat[:, pl.ds(pl.multiple_of((base + tiles) * LANES, LANES), LANES)] = last
        return 0

    lax.fori_loop(0, groups, place, 0)

    def read_flat(x):
        return flat[:, pl.ds(pl.multiple_of(x * size_y, size_y), size_y)]

    def read(x):
        return grid[x]

    def write(x, value):
        grid[x] = value

    sweep(read_flat, write, kx, ky, size_x, size_y)
    for repeat in range(STEPS - 1):
        sweep(read, write, kx, ky, size_x, size_y)

    def back(b, _):
        first = pl.multiple_of(b * 8, 8)
        out[0, :, pl.ds(first, 8), :] = jnp.swapaxes(grid[pl.ds(first, 8)], 0, 1)
        return 0

    lax.fori_loop(0, size_x // 8, back, 0, unroll=2)


def body(control, diffusivity, perturb, vertical_filter, sub_widths, obs_raw, obs_counts, obs_rinv):
    members, levels_here, size_x, size_y = control.shape
    columns = size_x * size_y
    capacity = perturb.shape[1]
    levels = perturb.shape[2]
    groups = sub_widths.shape[0]
    obs_cap = obs_raw.shape[1]
    part = capacity // PARTS
    half = part // 2
    n_mem = lax.axis_size("mem")
    me = lax.axis_index("lev")
    mem = lax.axis_index("mem")
    core = mem % 2
    starts = (jnp.cumsum(sub_widths) - sub_widths).astype(jnp.int32)
    info = jnp.stack([me, core]).astype(jnp.int32)
    smem = pl.BlockSpec(memory_space=pltpu.SMEM)
    params = pltpu.CompilerParams(vmem_limit_bytes=56 << 20)
    flat_width = columns + capacity + LANES
    piece_shape = jax.ShapeDtypeStruct((levels_here, part), F32)
    steps = levels_here // GROUP

    results = pl.pallas_call(
        functools.partial(forward_kernel, size_x, size_y, groups, capacity),
        grid=(steps,),
        in_specs=[
            smem,
            smem,
            pl.BlockSpec((1, GROUP, size_x, size_y), lambda g: (0, g, 0, 0)),
            pl.BlockSpec((GROUP, size_x, size_y), lambda g: (g, 0, 0)),
        ],
        out_specs=[pl.BlockSpec((size_x, GROUP, size_y), lambda g: (0, g, 0))]
        + [pl.BlockSpec((GROUP, part), lambda g: (g, 0))] * (groups * PARTS),
        out_shape=[jax.ShapeDtypeStruct((size_x, levels_here, size_y), F32)] + [piece_shape] * (groups * PARTS),
        scratch_shapes=[
            pltpu.VMEM((size_x, GROUP, size_y), F32),
            pltpu.VMEM((GROUP, flat_width), F32),
            pltpu.VMEM((size_x, GROUP, size_y), F32),
            pltpu.VMEM((size_x, GROUP, size_y), F32),
        ],
        compiler_params=params,
        name="smooth_and_cut",
    )(starts, info, control, diffusivity)
    diff = results[0]
    outgoing = results[1:]

    width = sub_widths[me]
    live = jnp.arange(obs_cap, dtype=jnp.int32) < obs_counts[me]
    slots = jnp.where(live, obs_raw[0] % width, -1)[None, :]
    order = jnp.bitwise_xor(me, jnp.arange(groups))
    vfilter = vertical_filter.reshape(levels, groups, levels_here)[:, order, :].reshape(levels, levels)

    rows_here = 256
    adjoint_pieces = []
    for c in range(PARTS):
        row0 = c * part + core * half
        w_info = jnp.stack([me, core, row0]).astype(jnp.int32)
        obs_weight = pl.pallas_call(
            functools.partial(observation_kernel, rows_here, obs_cap),
            grid=(half // rows_here,),
            in_specs=[
                smem,
                pl.BlockSpec((1, obs_cap), lambda g: (0, 0)),
                pl.BlockSpec((1, obs_cap, levels), lambda g: (0, 0, 0)),
            ],
            out_specs=pl.BlockSpec((rows_here, levels), lambda g: (g, 0)),
            out_shape=jax.ShapeDtypeStruct((half, levels), F32),
            scratch_shapes=[pltpu.VMEM((obs_cap, 2 * levels), BF16)],
            compiler_params=params,
            cost_estimate=pl.CostEstimate(
                flops=4 * half * obs_cap * levels, bytes_accessed=4 * obs_cap * levels, transcendentals=0
            ),
            name="observation_weights",
        )(w_info, slots, obs_rinv)

        pieces = [outgoing[c * groups]]
        for d in range(1, groups):
            pieces.append(lax.ppermute(outgoing[c * groups + d], "lev", flip_pairs(groups, d)))
        whole = pl.BlockSpec((levels_here, part), lambda g: (0, 0))
        chunk = pl.BlockSpec((1, part, levels), lambda g, c=c: (0, c, 0))
        square = pl.BlockSpec((levels, levels), lambda g: (0, 0))
        half_block = pl.BlockSpec((half, levels), lambda g: (0, 0))
        half_shape = jax.ShapeDtypeStruct((half, levels), F32)
        cost = pl.CostEstimate(
            flops=6 * part * levels * levels, bytes_accessed=12 * part * levels, transcendentals=0
        )
        keep, send = pl.pallas_call(
            functools.partial(filter_kernel, groups),
            grid=(1,),
            in_specs=[smem, square, chunk] + [whole] * groups,
            out_specs=[half_block, half_block],
            out_shape=[half_shape, half_shape],
            compiler_params=params,
            cost_estimate=cost,
            name="filter_forward",
        )(info, vfilter, perturb, *pieces)
        total = keep + lax.ppermute(send, "mem", flip_pairs(n_mem, 1))
        bit = 2
        while bit < n_mem:
            total = total + lax.ppermute(total, "mem", flip_pairs(n_mem, bit))
            bit *= 2
        adj_mine = total * obs_weight
        adj_other = lax.ppermute(adj_mine, "mem", flip_pairs(n_mem, 1))
        back = pl.pallas_call(
            functools.partial(back_kernel, groups),
            grid=(1,),
            in_specs=[smem, square, chunk, half_block, half_block],
            out_specs=[whole] * groups,
            out_shape=[piece_shape] * groups,
            compiler_params=params,
            cost_estimate=cost,
            name="filter_backward",
        )(info, vfilter, perturb, adj_mine, adj_other)
        adjoint_pieces.append(back[0])
        for d in range(1, groups):
            adjoint_pieces.append(lax.ppermute(back[d], "lev", flip_pairs(groups, d)))

    return pl.pallas_call(
        functools.partial(backward_kernel, size_x, size_y, groups, capacity),
        grid=(steps,),
        in_specs=[
            smem,
            smem,
            pl.BlockSpec((size_x, GROUP, size_y), lambda g: (0, g, 0)),
        ]
        + [pl.BlockSpec(memory_space=pl.ANY)] * (groups * PARTS),
        out_specs=pl.BlockSpec((1, GROUP, size_x, size_y), lambda g: (0, g, 0, 0)),
        out_shape=jax.ShapeDtypeStruct((members, levels_here, size_x, size_y), F32),
        scratch_shapes=[
            pltpu.VMEM((groups, GROUP, capacity), F32),
            pltpu.VMEM((GROUP, flat_width), F32),
            pltpu.VMEM((size_x, GROUP, size_y), F32),
            pltpu.VMEM((size_x, GROUP, size_y), F32),
            pltpu.VMEM((size_x, GROUP, size_y), F32),
            pltpu.SemaphoreType.DMA((groups * PARTS,)),
        ],
        compiler_params=params,
        name="place_and_smooth",
    )(starts, info, diff, *adjoint_pieces)


def solution(mesh):
    return jax.shard_map(
        body,
        mesh=mesh,
        in_specs=(
            P("mem", "lev", None, None),
            P("lev", None, None),
            P("mem", "lev", None),
            P(),
            P(),
            P("lev", None),
            P(),
            P("lev", None, None),
        ),
        out_specs=P("mem", "lev", None, None),
        check_vma=False,
    )
```

```python
import functools

import jax
import jax.numpy as jnp
from jax import lax
from jax.experimental import pallas as pl
from jax.experimental.pallas import tpu as pltpu
from jax.sharding import PartitionSpec as P

STEPS = 4
PARTS = 3
LANES = 128
GROUP = 8
F32 = jnp.float32
BF16 = jnp.bfloat16


def flip_pairs(size, bit):
    return [(i, i ^ bit) for i in range(size)]


def transpose_in(src, dst, size_x):
    def step(b, _):
        first = pl.multiple_of(b * 8, 8)
        dst[pl.ds(first, 8)] = jnp.swapaxes(src[:, pl.ds(first, 8), :], 0, 1)
        return 0

    lax.fori_loop(0, size_x // 8, step, 0, unroll=2)


def faces(diff, face_x, face_up, face_down, size_x, size_y):
    lane = lax.broadcasted_iota(jnp.int32, (1, GROUP, size_y), 2)
    rows = 16

    def step(b, _):
        first = pl.multiple_of(b * rows, rows)
        here = diff[pl.ds(first, rows)]
        beyond = diff[pl.ds(jnp.minimum(first + rows, size_x - 1), 1)]
        ahead = jnp.concatenate([here[1:], beyond], axis=0)
        row = first + lax.broadcasted_iota(jnp.int32, (rows, GROUP, size_y), 0)
        face_x[pl.ds(first, rows)] = jnp.where(row < size_x - 1, 0.5 * (here + ahead), 0.0)
        up = 0.5 * (here + pltpu.roll(here, size_y - 1, 2))
        face_up[pl.ds(first, rows)] = jnp.where(lane < size_y - 1, up, 0.0)
        down = 0.5 * (here + pltpu.roll(here, 1, 2))
        face_down[pl.ds(first, rows)] = jnp.where(lane > 0, down, 0.0)
        return 0

    lax.fori_loop(0, size_x // rows, step, 0)


def sweep(read, write, face_x, face_up, face_down, size_x, size_y):
    rows = 8

    def step(b, flux_before):
        first = pl.multiple_of(b * rows, rows)
        here = read(first, rows)
        beyond = read(jnp.minimum(first + rows, size_x - 1), 1)
        ahead = jnp.concatenate([here[1:], beyond], axis=0)
        flux_x = face_x[pl.ds(first, rows)] * (ahead - here)
        flux_up = face_up[pl.ds(first, rows)] * (pltpu.roll(here, size_y - 1, 2) - here)
        flux_down = face_down[pl.ds(first, rows)] * (here - pltpu.roll(here, 1, 2))
        behind = jnp.concatenate([flux_before, flux_x[:-1]], axis=0)
        write(first, rows, here + (flux_x - behind) + (flux_up - flux_down))
        return flux_x[-1:]

    lax.fori_loop(0, size_x // rows, step, jnp.zeros((1, GROUP, size_y), F32), unroll=4)


def on_grid(grid):
    def read(first, rows):
        return grid[pl.ds(first, rows)]

    def write(first, rows, value):
        grid[pl.ds(first, rows)] = value

    return read, write


def on_flat(flat, size_y):
    def at(x):
        return pl.ds(pl.multiple_of(x * size_y, size_y), size_y)

    def read(first, rows):
        return jnp.stack([flat[:, at(first + i)] for i in range(rows)], axis=0)

    def write(first, rows, value):
        for i in range(rows):
            flat[:, at(first + i)] = value[i]

    return read, write


def forward_kernel(size_x, size_y, groups, capacity, starts, info, control, diffusivity, diff_out, *rest):
    outs = rest[: groups * PARTS]
    flat, one, two, *face_refs = rest[groups * PARTS :]
    columns = size_x * size_y
    part = capacity // PARTS
    transpose_in(diffusivity, diff_out, size_x)
    faces(diff_out, *face_refs, size_x, size_y)
    transpose_in(control.at[0], one, size_x)
    stages = [on_grid((one, two)[i % 2]) for i in range(STEPS)] + [on_flat(flat, size_y)]
    for i in range(STEPS):
        sweep(stages[i][0], stages[i + 1][1], *face_refs, size_x, size_y)
    flat[:, columns:] = jnp.zeros((GROUP, flat.shape[1] - columns), F32)

    lane = lax.broadcasted_iota(jnp.int32, (GROUP, LANES), 1)
    me = info[0]
    tiles = part // LANES
    for d in range(groups):
        start = starts[jnp.bitwise_xor(me, d)]
        base = start // LANES
        shift = start - base * LANES
        back = lax.rem(LANES - shift, LANES)
        low = lane < LANES - shift
        for c in range(PARTS):
            out = outs[c * groups + d]
            begin = base + c * tiles

            def load(t):
                at = pl.multiple_of((begin + t) * LANES, LANES)
                return pltpu.roll(flat[:, pl.ds(at, LANES)], back, 1)

            now = load(0)
            for t in range(tiles):
                later = load(t + 1)
                out[:, t * LANES : (t + 1) * LANES] = jnp.where(low, now, later)
                now = later


def split3(value):
    high = value.astype(BF16)
    return high, (value - high.astype(F32)).astype(BF16)


def dot3(a, b, dims):
    ah, al = split3(a)
    bh, bl = split3(b)
    dot = functools.partial(lax.dot_general, dimension_numbers=(dims, ((), ())), preferred_element_type=F32)
    return dot(ah, bh) + (dot(ah, bl) + dot(al, bh))


def observation_kernel(rows_here, obs_cap, info, slots, rinv, out, split):
    step = pl.program_id(0)

    @pl.when(step == 0)
    def _():
        values = rinv[0]
        high = values.astype(BF16)
        split[:, :LANES] = high
        split[:, LANES:] = (values - high.astype(F32)).astype(BF16)

    first = info[2] + step * rows_here
    block = 512
    row = first + lax.broadcasted_iota(jnp.int32, (rows_here, block), 0)

    def add(b, total):
        at = pl.multiple_of(b * block, block)
        hit = row == slots[:, pl.ds(at, block)]
        onehot = jnp.where(hit, 1.0, 0.0).astype(BF16)
        return total + jnp.dot(onehot, split[pl.ds(at, block), :], preferred_element_type=F32)

    total = lax.fori_loop(0, obs_cap // block, add, jnp.zeros((rows_here, 2 * LANES), F32))
    out[...] = total[:, :LANES] + total[:, LANES:]


def filter_kernel(groups, info, vfilter, perturb, *rest):
    pieces = rest[:groups]
    keep, send = rest[groups:]
    half = keep.shape[0]
    width = 256
    mine = info[1]
    for which, out in ((mine, keep), (1 - mine, send)):

        def step(b, _):
            at = pl.multiple_of(which * half + b * width, width)
            slab = jnp.concatenate([piece[:, pl.ds(at, width)] for piece in pieces], axis=0)
            filtered = dot3(slab.T, vfilter[...], ((1,), (1,)))
            out[pl.ds(pl.multiple_of(b * width, width), width), :] = (
                perturb[0, pl.ds(at, width), :] * filtered
            )
            return 0

        lax.fori_loop(0, half // width, step, 0, unroll=2)


def back_kernel(groups, info, vfilter, perturb, adj_mine, adj_other, *pieces):
    half = adj_mine.shape[0]
    width = 256
    levels = pieces[0].shape[0]
    mine = info[1]
    for which, adj in ((mine, adj_mine), (1 - mine, adj_other)):

        def step(b, _):
            at = pl.multiple_of(which * half + b * width, width)
            weighted = perturb[0, pl.ds(at, width), :] * adj[pl.ds(pl.multiple_of(b * width, width), width), :]
            result = dot3(vfilter[...], weighted, ((0,), (1,)))
            for d in range(groups):
                pieces[d][:, pl.ds(at, width)] = result[d * levels : (d + 1) * levels]
            return 0

        lax.fori_loop(0, half // width, step, 0, unroll=2)


def backward_kernel(size_x, size_y, groups, capacity, starts, info, diff, *rest):
    ins = rest[: groups * PARTS]
    out, staging, flat, one, two, *face_refs, sem = rest[groups * PARTS :]
    part = capacity // PARTS
    me = info[0]
    step_id = pl.program_id(0)
    level = pl.multiple_of(step_id * GROUP, GROUP)
    copies = []
    for c in range(PARTS):
        for d in range(groups):
            copies.append(
                pltpu.make_async_copy(
                    ins[c * groups + d].at[pl.ds(level, GROUP), :],
                    staging.at[jnp.bitwise_xor(me, d), :, pl.ds(c * part, part)],
                    sem.at[c * groups + d],
                )
            )
    for copy in copies:
        copy.start()
    faces(diff, *face_refs, size_x, size_y)
    for copy in copies:
        copy.wait()

    lane = lax.broadcasted_iota(jnp.int32, (GROUP, LANES), 1)
    tiles = capacity // LANES
    some = 8

    def place(j, _):
        start = starts[j]
        base = start // LANES
        shift = start - base * LANES
        high = lane >= shift

        def several(b, before):
            for t in range(some):
                at = pl.multiple_of((b * some + t) * LANES, LANES)
                to = pl.multiple_of((base + b * some + t) * LANES, LANES)
                here = pltpu.roll(staging[j, :, pl.ds(at, LANES)], shift, 1)
                flat[:, pl.ds(to, LANES)] = jnp.where(high, here, before)
                before = here
            return before

        existing = flat[:, pl.ds(pl.multiple_of(base * LANES, LANES), LANES)]
        last = lax.fori_loop(0, tiles // some, several, existing)
        flat[:, pl.ds(pl.multiple_of((base + tiles) * LANES, LANES), LANES)] = last
        return 0

    lax.fori_loop(0, groups, place, 0)

    stages = [on_flat(flat, size_y)] + [on_grid((one, two)[i % 2]) for i in range(STEPS)]
    for i in range(STEPS):
        sweep(stages[i][0], stages[i + 1][1], *face_refs, size_x, size_y)
    grid = (one, two)[(STEPS - 1) % 2]

    def back(b, _):
        first = pl.multiple_of(b * 8, 8)
        out[0, :, pl.ds(first, 8), :] = jnp.swapaxes(grid[pl.ds(first, 8)], 0, 1)
        return 0

    lax.fori_loop(0, size_x // 8, back, 0, unroll=2)


def body(control, diffusivity, perturb, vertical_filter, sub_widths, obs_raw, obs_counts, obs_rinv):
    members, levels_here, size_x, size_y = control.shape
    columns = size_x * size_y
    capacity = perturb.shape[1]
    levels = perturb.shape[2]
    groups = sub_widths.shape[0]
    obs_cap = obs_raw.shape[1]
    part = capacity // PARTS
    half = part // 2
    n_mem = lax.axis_size("mem")
    me = lax.axis_index("lev")
    mem = lax.axis_index("mem")
    core = mem % 2
    starts = (jnp.cumsum(sub_widths) - sub_widths).astype(jnp.int32)
    info = jnp.stack([me, core]).astype(jnp.int32)
    smem = pl.BlockSpec(memory_space=pltpu.SMEM)
    params = pltpu.CompilerParams(vmem_limit_bytes=56 << 20)
    flat_width = columns + capacity + LANES
    piece_shape = jax.ShapeDtypeStruct((levels_here, part), F32)
    steps = levels_here // GROUP

    results = pl.pallas_call(
        functools.partial(forward_kernel, size_x, size_y, groups, capacity),
        grid=(steps,),
        in_specs=[
            smem,
            smem,
            pl.BlockSpec((1, GROUP, size_x, size_y), lambda g: (0, g, 0, 0)),
            pl.BlockSpec((GROUP, size_x, size_y), lambda g: (g, 0, 0)),
        ],
        out_specs=[pl.BlockSpec((size_x, GROUP, size_y), lambda g: (0, g, 0))]
        + [pl.BlockSpec((GROUP, part), lambda g: (g, 0))] * (groups * PARTS),
        out_shape=[jax.ShapeDtypeStruct((size_x, levels_here, size_y), F32)] + [piece_shape] * (groups * PARTS),
        scratch_shapes=[
            pltpu.VMEM((GROUP, flat_width), F32),
        ]
        + [pltpu.VMEM((size_x, GROUP, size_y), F32)] * 5,
        compiler_params=params,
        name="smooth_and_cut",
    )(starts, info, control, diffusivity)
    diff = results[0]
    outgoing = results[1:]

    width = sub_widths[me]
    live = jnp.arange(obs_cap, dtype=jnp.int32) < obs_counts[me]
    slots = jnp.where(live, obs_raw[0] % width, -1)[None, :]
    order = jnp.bitwise_xor(me, jnp.arange(groups))
    vfilter = vertical_filter.reshape(levels, groups, levels_here)[:, order, :].reshape(levels, levels)

    rows_here = 256
    adjoint_pieces = []
    for c in range(PARTS):
        row0 = c * part + core * half
        w_info = jnp.stack([me, core, row0]).astype(jnp.int32)
        obs_weight = pl.pallas_call(
            functools.partial(observation_kernel, rows_here, obs_cap),
            grid=(half // rows_here,),
            in_specs=[
                smem,
                pl.BlockSpec((1, obs_cap), lambda g: (0, 0)),
                pl.BlockSpec((1, obs_cap, levels), lambda g: (0, 0, 0)),
            ],
            out_specs=pl.BlockSpec((rows_here, levels), lambda g: (g, 0)),
            out_shape=jax.ShapeDtypeStruct((half, levels), F32),
            scratch_shapes=[pltpu.VMEM((obs_cap, 2 * levels), BF16)],
            compiler_params=params,
            cost_estimate=pl.CostEstimate(
                flops=4 * half * obs_cap * levels, bytes_accessed=4 * obs_cap * levels, transcendentals=0
            ),
            name="observation_weights",
        )(w_info, slots, obs_rinv)

        pieces = [outgoing[c * groups]]
        for d in range(1, groups):
            pieces.append(lax.ppermute(outgoing[c * groups + d], "lev", flip_pairs(groups, d)))
        whole = pl.BlockSpec((levels_here, part), lambda g: (0, 0))
        chunk = pl.BlockSpec((1, part, levels), lambda g, c=c: (0, c, 0))
        square = pl.BlockSpec((levels, levels), lambda g: (0, 0))
        half_block = pl.BlockSpec((half, levels), lambda g: (0, 0))
        half_shape = jax.ShapeDtypeStruct((half, levels), F32)
        cost = pl.CostEstimate(
            flops=6 * part * levels * levels, bytes_accessed=12 * part * levels, transcendentals=0
        )
        keep, send = pl.pallas_call(
            functools.partial(filter_kernel, groups),
            grid=(1,),
            in_specs=[smem, square, chunk] + [whole] * groups,
            out_specs=[half_block, half_block],
            out_shape=[half_shape, half_shape],
            compiler_params=params,
            cost_estimate=cost,
            name="filter_forward",
        )(info, vfilter, perturb, *pieces)
        total = keep + lax.ppermute(send, "mem", flip_pairs(n_mem, 1))
        bit = 2
        while bit < n_mem:
            total = total + lax.ppermute(total, "mem", flip_pairs(n_mem, bit))
            bit *= 2
        adj_mine = total * obs_weight
        adj_other = lax.ppermute(adj_mine, "mem", flip_pairs(n_mem, 1))
        back = pl.pallas_call(
            functools.partial(back_kernel, groups),
            grid=(1,),
            in_specs=[smem, square, chunk, half_block, half_block],
            out_specs=[whole] * groups,
            out_shape=[piece_shape] * groups,
            compiler_params=params,
            cost_estimate=cost,
            name="filter_backward",
        )(info, vfilter, perturb, adj_mine, adj_other)
        adjoint_pieces.append(back[0])
        for d in range(1, groups):
            adjoint_pieces.append(lax.ppermute(back[d], "lev", flip_pairs(groups, d)))

    return pl.pallas_call(
        functools.partial(backward_kernel, size_x, size_y, groups, capacity),
        grid=(steps,),
        in_specs=[
            smem,
            smem,
            pl.BlockSpec((size_x, GROUP, size_y), lambda g: (0, g, 0)),
        ]
        + [pl.BlockSpec(memory_space=pl.ANY)] * (groups * PARTS),
        out_specs=pl.BlockSpec((1, GROUP, size_x, size_y), lambda g: (0, g, 0, 0)),
        out_shape=jax.ShapeDtypeStruct((members, levels_here, size_x, size_y), F32),
        scratch_shapes=[
            pltpu.VMEM((groups, GROUP, capacity), F32),
            pltpu.VMEM((GROUP, flat_width), F32),
        ]
        + [pltpu.VMEM((size_x, GROUP, size_y), F32)] * 5
        + [pltpu.SemaphoreType.DMA((groups * PARTS,))],
        compiler_params=params,
        name="place_and_smooth",
    )(starts, info, diff, *adjoint_pieces)


def solution(mesh):
    return jax.shard_map(
        body,
        mesh=mesh,
        in_specs=(
            P("mem", "lev", None, None),
            P("lev", None, None),
            P("mem", "lev", None),
            P(),
            P(),
            P("lev", None),
            P(),
            P("lev", None, None),
        ),
        out_specs=P("mem", "lev", None, None),
        check_vma=False,
    )
```

```python
import functools

import jax
import jax.numpy as jnp
from jax import lax
from jax.experimental import pallas as pl
from jax.experimental.pallas import tpu as pltpu
from jax.sharding import PartitionSpec as P

STEPS = 4
PARTS = 2
LANES = 128
GROUP = 8
F32 = jnp.float32
BF16 = jnp.bfloat16


def flip_pairs(size, bit):
    return [(i, i ^ bit) for i in range(size)]


def transpose_in(src, dst, size_x):
    def step(b, _):
        first = pl.multiple_of(b * 8, 8)
        dst[pl.ds(first, 8)] = jnp.swapaxes(src[:, pl.ds(first, 8), :], 0, 1)
        return 0

    lax.fori_loop(0, size_x // 8, step, 0, unroll=2)


def faces(diff, face_x, face_up, face_down, size_x, size_y):
    lane = lax.broadcasted_iota(jnp.int32, (1, GROUP, size_y), 2)
    rows = 16

    def step(b, _):
        first = pl.multiple_of(b * rows, rows)
        here = diff[pl.ds(first, rows)]
        beyond = diff[pl.ds(jnp.minimum(first + rows, size_x - 1), 1)]
        ahead = jnp.concatenate([here[1:], beyond], axis=0)
        row = first + lax.broadcasted_iota(jnp.int32, (rows, GROUP, size_y), 0)
        face_x[pl.ds(first, rows)] = jnp.where(row < size_x - 1, 0.5 * (here + ahead), 0.0)
        up = 0.5 * (here + pltpu.roll(here, size_y - 1, 2))
        face_up[pl.ds(first, rows)] = jnp.where(lane < size_y - 1, up, 0.0)
        down = 0.5 * (here + pltpu.roll(here, 1, 2))
        face_down[pl.ds(first, rows)] = jnp.where(lane > 0, down, 0.0)
        return 0

    lax.fori_loop(0, size_x // rows, step, 0)


def sweep(read, write, face_x, face_up, face_down, size_x, size_y):
    rows = 8

    def step(b, flux_before):
        first = pl.multiple_of(b * rows, rows)
        here = read(first, rows)
        beyond = read(jnp.minimum(first + rows, size_x - 1), 1)
        ahead = jnp.concatenate([here[1:], beyond], axis=0)
        flux_x = face_x[pl.ds(first, rows)] * (ahead - here)
        flux_up = face_up[pl.ds(first, rows)] * (pltpu.roll(here, size_y - 1, 2) - here)
        flux_down = face_down[pl.ds(first, rows)] * (here - pltpu.roll(here, 1, 2))
        behind = jnp.concatenate([flux_before, flux_x[:-1]], axis=0)
        write(first, rows, here + (flux_x - behind) + (flux_up - flux_down))
        return flux_x[-1:]

    lax.fori_loop(0, size_x // rows, step, jnp.zeros((1, GROUP, size_y), F32), unroll=4)


def on_grid(grid):
    def read(first, rows):
        return grid[pl.ds(first, rows)]

    def write(first, rows, value):
        grid[pl.ds(first, rows)] = value

    return read, write


def on_flat(flat, size_y):
    def at(x):
        return pl.ds(pl.multiple_of(x * size_y, size_y), size_y)

    def read(first, rows):
        return jnp.stack([flat[:, at(first + i)] for i in range(rows)], axis=0)

    def write(first, rows, value):
        for i in range(rows):
            flat[:, at(first + i)] = value[i]

    return read, write


def start_of(widths, j):
    return lax.fori_loop(0, j, lambda k, total: total + widths[k], jnp.int32(0))


def forward_kernel(size_x, size_y, groups, capacity, widths, control, diffusivity, diff_out, *rest):
    outs = rest[: groups * PARTS]
    flat, one, two, *face_refs = rest[groups * PARTS :]
    columns = size_x * size_y
    part = capacity // PARTS
    transpose_in(diffusivity, diff_out, size_x)
    faces(diff_out, *face_refs, size_x, size_y)
    transpose_in(control.at[0], one, size_x)
    stages = [on_grid((one, two)[i % 2]) for i in range(STEPS)] + [on_flat(flat, size_y)]
    for i in range(STEPS):
        sweep(stages[i][0], stages[i + 1][1], *face_refs, size_x, size_y)
    flat[:, columns:] = jnp.zeros((GROUP, flat.shape[1] - columns), F32)

    lane = lax.broadcasted_iota(jnp.int32, (GROUP, LANES), 1)
    me = lax.axis_index("lev")
    tiles = part // LANES
    for d, turn in enumerate(turns_of(groups)):
        start = start_of(widths, jnp.bitwise_xor(me, turn))
        base = start // LANES
        shift = start - base * LANES
        back = lax.rem(LANES - shift, LANES)
        low = lane < LANES - shift
        for c in range(PARTS):
            out = outs[c * groups + d]
            begin = base + c * tiles

            def load(t):
                at = pl.multiple_of((begin + t) * LANES, LANES)
                return pltpu.roll(flat[:, pl.ds(at, LANES)], back, 1)

            now = load(0)
            for t in range(tiles):
                later = load(t + 1)
                out[:, t * LANES : (t + 1) * LANES] = jnp.where(low, now, later)
                now = later


def turns_of(groups):
    return [0] + list(range(groups // 2, groups)) + list(range(groups // 2 - 1, 0, -1))


def split2(value):
    high = value.astype(BF16)
    return high, (value - high.astype(F32)).astype(BF16)


def dot3(a, b, dims):
    ah, al = split2(a)
    bh, bl = split2(b)
    dot = functools.partial(lax.dot_general, dimension_numbers=(dims, ((), ())), preferred_element_type=F32)
    return dot(ah, bh) + (dot(ah, bl) + dot(al, bh))


def observation_kernel(part_rows, index, obs_cap, slots, rinv, out, split):
    step = pl.program_id(0)
    rows_here, levels = out.shape

    @pl.when(step == 0)
    def _():
        high, low = split2(rinv[0])
        split[:, :levels] = high
        split[:, levels:] = low

    core = lax.axis_index("mem") % 2
    first = index * part_rows + core * (part_rows // 2) + step * rows_here
    row = first + lax.broadcasted_iota(jnp.int32, (rows_here, obs_cap), 0)
    onehot = jnp.where(row == slots[...], 1.0, 0.0).astype(BF16)
    total = jnp.dot(onehot, split[...], preferred_element_type=F32)
    out[...] = total[:, :levels] + total[:, levels:]


def filter_kernel(groups, vfilter, perturb, *rest):
    pieces = rest[:groups]
    keep, send = rest[groups:]
    half = keep.shape[0]
    width = 256
    mine = lax.axis_index("mem") % 2
    for which, out in ((mine, keep), (1 - mine, send)):

        def step(b, _):
            at = pl.multiple_of(which * half + b * width, width)
            slab = jnp.concatenate([piece[:, pl.ds(at, width)] for piece in pieces], axis=0)
            filtered = dot3(slab.T, vfilter[...], ((1,), (1,)))
            out[pl.ds(pl.multiple_of(b * width, width), width), :] = (
                perturb[0, pl.ds(at, width), :] * filtered
            )
            return 0

        lax.fori_loop(0, half // width, step, 0, unroll=2)


def back_kernel(groups, vfilter, perturb, adj_mine, adj_other, *pieces):
    half = adj_mine.shape[0]
    width = 256
    levels = pieces[0].shape[0]
    mine = lax.axis_index("mem") % 2
    for which, adj in ((mine, adj_mine), (1 - mine, adj_other)):

        def step(b, _):
            at = pl.multiple_of(which * half + b * width, width)
            weighted = perturb[0, pl.ds(at, width), :] * adj[pl.ds(pl.multiple_of(b * width, width), width), :]
            result = dot3(vfilter[...], weighted, ((0,), (1,)))
            for d in range(groups):
                pieces[d][:, pl.ds(at, width)] = result[d * levels : (d + 1) * levels]
            return 0

        lax.fori_loop(0, half // width, step, 0, unroll=2)


def backward_kernel(size_x, size_y, groups, capacity, widths, diff, *rest):
    ins = rest[: groups * PARTS]
    out, staging, flat, one, two, *face_refs, sem = rest[groups * PARTS :]
    part = capacity // PARTS
    me = lax.axis_index("lev")
    step_id = pl.program_id(0)
    level = pl.multiple_of(step_id * GROUP, GROUP)
    copies = []
    for c in range(PARTS):
        for d, turn in enumerate(turns_of(groups)):
            copies.append(
                pltpu.make_async_copy(
                    ins[c * groups + d].at[pl.ds(level, GROUP), :],
                    staging.at[jnp.bitwise_xor(me, turn), :, pl.ds(c * part, part)],
                    sem.at[c * groups + d],
                )
            )
    for copy in copies:
        copy.start()
    faces(diff, *face_refs, size_x, size_y)
    for copy in copies:
        copy.wait()

    lane = lax.broadcasted_iota(jnp.int32, (GROUP, LANES), 1)
    tiles = capacity // LANES
    some = 8

    def place(j, _):
        start = start_of(widths, j)
        base = start // LANES
        shift = start - base * LANES
        high = lane >= shift

        def several(b, before):
            for t in range(some):
                at = pl.multiple_of((b * some + t) * LANES, LANES)
                to = pl.multiple_of((base + b * some + t) * LANES, LANES)
                here = pltpu.roll(staging[j, :, pl.ds(at, LANES)], shift, 1)
                flat[:, pl.ds(to, LANES)] = jnp.where(high, here, before)
                before = here
            return before

        existing = flat[:, pl.ds(pl.multiple_of(base * LANES, LANES), LANES)]
        last = lax.fori_loop(0, tiles // some, several, existing)
        flat[:, pl.ds(pl.multiple_of((base + tiles) * LANES, LANES), LANES)] = last
        return 0

    lax.fori_loop(0, groups, place, 0)

    stages = [on_flat(flat, size_y)] + [on_grid((one, two)[i % 2]) for i in range(STEPS)]
    for i in range(STEPS):
        sweep(stages[i][0], stages[i + 1][1], *face_refs, size_x, size_y)
    grid = (one, two)[(STEPS - 1) % 2]

    def back(b, _):
        first = pl.multiple_of(b * 8, 8)
        out[0, :, pl.ds(first, 8), :] = jnp.swapaxes(grid[pl.ds(first, 8)], 0, 1)
        return 0

    lax.fori_loop(0, size_x // 8, back, 0, unroll=2)


def after(value, *others):
    return lax.optimization_barrier((value,) + others)[0]


def body(control, diffusivity, perturb, vertical_filter, sub_widths, obs_raw, obs_counts, obs_rinv):
    members, levels_here, size_x, size_y = control.shape
    columns = size_x * size_y
    capacity = perturb.shape[1]
    levels = perturb.shape[2]
    groups = sub_widths.shape[0]
    obs_cap = obs_raw.shape[1]
    part = capacity // PARTS
    half = part // 2
    n_mem = lax.axis_size("mem")
    me = lax.axis_index("lev")
    smem = pl.BlockSpec(memory_space=pltpu.SMEM)
    params = pltpu.CompilerParams(vmem_limit_bytes=56 << 20)
    flat_width = columns + capacity + LANES
    piece_shape = jax.ShapeDtypeStruct((levels_here, part), F32)
    steps = levels_here // GROUP

    results = pl.pallas_call(
        functools.partial(forward_kernel, size_x, size_y, groups, capacity),
        grid=(steps,),
        in_specs=[
            smem,
            pl.BlockSpec((1, GROUP, size_x, size_y), lambda g: (0, g, 0, 0)),
            pl.BlockSpec((GROUP, size_x, size_y), lambda g: (g, 0, 0)),
        ],
        out_specs=[pl.BlockSpec((size_x, GROUP, size_y), lambda g: (0, g, 0))]
        + [pl.BlockSpec((GROUP, part), lambda g: (g, 0))] * (groups * PARTS),
        out_shape=[jax.ShapeDtypeStruct((size_x, levels_here, size_y), F32)] + [piece_shape] * (groups * PARTS),
        scratch_shapes=[
            pltpu.VMEM((GROUP, flat_width), F32),
        ]
        + [pltpu.VMEM((size_x, GROUP, size_y), F32)] * 5,
        compiler_params=params,
        name="smooth_and_cut",
    )(sub_widths, control, diffusivity)
    diff = results[0]
    outgoing = [results[1 + c * groups : 1 + (c + 1) * groups] for c in range(PARTS)]

    width = sub_widths[me]
    live = jnp.arange(obs_cap, dtype=jnp.int32) < obs_counts[me]
    slots = jnp.where(live, obs_raw[0] % width, -1)[None, :]
    turns = turns_of(groups)
    order = jnp.bitwise_xor(me, jnp.array(turns, jnp.int32))
    vfilter = vertical_filter.reshape(levels, groups, levels_here)[:, order, :].reshape(levels, levels)

    whole = pl.BlockSpec((levels_here, part), lambda g: (0, 0))
    square = pl.BlockSpec((levels, levels), lambda g: (0, 0))
    half_block = pl.BlockSpec((half, levels), lambda g: (0, 0))
    half_shape = jax.ShapeDtypeStruct((half, levels), F32)
    cost = pl.CostEstimate(flops=0, bytes_accessed=0, transcendentals=0)
    rows_here = 256

    def weights(c, slots):
        return pl.pallas_call(
            functools.partial(observation_kernel, part, c, obs_cap),
            grid=(half // rows_here,),
            in_specs=[
                pl.BlockSpec((1, obs_cap), lambda g: (0, 0)),
                pl.BlockSpec((1, obs_cap, levels), lambda g: (0, 0, 0)),
            ],
            out_specs=pl.BlockSpec((rows_here, levels), lambda g: (g, 0)),
            out_shape=jax.ShapeDtypeStruct((half, levels), F32),
            scratch_shapes=[pltpu.VMEM((obs_cap, 2 * levels), BF16)],
            compiler_params=params,
            cost_estimate=cost,
            name="observation_weights",
        )(slots, obs_rinv)

    def filter_forward(c, vfilter, pieces):
        chunk = pl.BlockSpec((1, part, levels), lambda g: (0, c, 0))
        return pl.pallas_call(
            functools.partial(filter_kernel, groups),
            grid=(1,),
            in_specs=[square, chunk] + [whole] * groups,
            out_specs=[half_block, half_block],
            out_shape=[half_shape, half_shape],
            compiler_params=params,
            cost_estimate=cost,
            name="filter_forward",
        )(vfilter, perturb, *pieces)

    def filter_backward(c, adj_mine, adj_other):
        chunk = pl.BlockSpec((1, part, levels), lambda g: (0, c, 0))
        return pl.pallas_call(
            functools.partial(back_kernel, groups),
            grid=(1,),
            in_specs=[square, chunk, half_block, half_block],
            out_specs=[whole] * groups,
            out_shape=[piece_shape] * groups,
            compiler_params=params,
            cost_estimate=cost,
            name="filter_backward",
        )(vfilter, perturb, adj_mine, adj_other)

    def exchange(pieces):
        return [pieces[0]] + [lax.ppermute(pieces[d], "lev", flip_pairs(groups, turns[d])) for d in range(1, groups)]

    def sum_members(keep, send, gate):
        total = keep + lax.ppermute(send, "mem", flip_pairs(n_mem, 1))
        bit = 2
        while bit < n_mem:
            other = lax.ppermute(total, "mem", flip_pairs(n_mem, bit))
            total = total + (after(other, *gate) if gate else other)
            bit *= 2
        return total

    def adjoint(total, obs_weight):
        mine = total * obs_weight
        return mine, lax.ppermute(mine, "mem", flip_pairs(n_mem, 1))

    got = [exchange(outgoing[c]) for c in range(PARTS)]
    slots = after(slots, got[0][1])
    weight = [weights(c, slots) for c in range(PARTS)]
    back = []
    gate_filter = []
    gate_sum = []
    for c in range(PARTS):
        gated = after(vfilter, *gate_filter) if gate_filter else vfilter
        keep, send = filter_forward(c, gated, got[c])
        mine, other = adjoint(sum_members(keep, send, gate_sum), weight[c])
        gate_filter = [mine] + weight
        pieces = exchange(filter_backward(c, mine, other))
        gate_sum = [pieces[3]]
        back += pieces

    return pl.pallas_call(
        functools.partial(backward_kernel, size_x, size_y, groups, capacity),
        grid=(steps,),
        in_specs=[
            smem,
            pl.BlockSpec((size_x, GROUP, size_y), lambda g: (0, g, 0)),
        ]
        + [pl.BlockSpec(memory_space=pl.ANY)] * (groups * PARTS),
        out_specs=pl.BlockSpec((1, GROUP, size_x, size_y), lambda g: (0, g, 0, 0)),
        out_shape=jax.ShapeDtypeStruct((members, levels_here, size_x, size_y), F32),
        scratch_shapes=[
            pltpu.VMEM((groups, GROUP, capacity), F32),
            pltpu.VMEM((GROUP, flat_width), F32),
        ]
        + [pltpu.VMEM((size_x, GROUP, size_y), F32)] * 5
        + [pltpu.SemaphoreType.DMA((groups * PARTS,))],
        compiler_params=params,
        name="place_and_smooth",
    )(sub_widths, diff, *back)


def solution(mesh):
    return jax.shard_map(
        body,
        mesh=mesh,
        in_specs=(
            P("mem", "lev", None, None),
            P("lev", None, None),
            P("mem", "lev", None),
            P(),
            P(),
            P("lev", None),
            P(),
            P("lev", None, None),
        ),
        out_specs=P("mem", "lev", None, None),
        check_vma=False,
    )
```

```python
import functools

import jax
import jax.numpy as jnp
from jax import lax
from jax.experimental import pallas as pl
from jax.experimental.pallas import tpu as pltpu
from jax.sharding import PartitionSpec as P

STEPS = 4
PARTS = 2
LANES = 128
GROUP = 8
F32 = jnp.float32
BF16 = jnp.bfloat16


def flip_pairs(size, bit):
    return [(i, i ^ bit) for i in range(size)]


def transpose_in(src, dst, size_x):
    def step(b, _):
        first = pl.multiple_of(b * 8, 8)
        dst[pl.ds(first, 8)] = jnp.swapaxes(src[:, pl.ds(first, 8), :], 0, 1)
        return 0

    lax.fori_loop(0, size_x // 8, step, 0, unroll=2)


def faces(diff, face_x, face_up, face_down, size_x, size_y):
    lane = lax.broadcasted_iota(jnp.int32, (1, GROUP, size_y), 2)
    rows = 16

    def step(b, _):
        first = pl.multiple_of(b * rows, rows)
        here = diff[pl.ds(first, rows)]
        beyond = diff[pl.ds(jnp.minimum(first + rows, size_x - 1), 1)]
        ahead = jnp.concatenate([here[1:], beyond], axis=0)
        row = first + lax.broadcasted_iota(jnp.int32, (rows, GROUP, size_y), 0)
        face_x[pl.ds(first, rows)] = jnp.where(row < size_x - 1, 0.5 * (here + ahead), 0.0)
        up = 0.5 * (here + pltpu.roll(here, size_y - 1, 2))
        face_up[pl.ds(first, rows)] = jnp.where(lane < size_y - 1, up, 0.0)
        down = 0.5 * (here + pltpu.roll(here, 1, 2))
        face_down[pl.ds(first, rows)] = jnp.where(lane > 0, down, 0.0)
        return 0

    lax.fori_loop(0, size_x // rows, step, 0)


def sweep(read, write, face_x, face_up, face_down, size_x, size_y):
    rows = 8

    def step(b, flux_before):
        first = pl.multiple_of(b * rows, rows)
        here = read(first, rows)
        beyond = read(jnp.minimum(first + rows, size_x - 1), 1)
        ahead = jnp.concatenate([here[1:], beyond], axis=0)
        flux_x = face_x[pl.ds(first, rows)] * (ahead - here)
        flux_up = face_up[pl.ds(first, rows)] * (pltpu.roll(here, size_y - 1, 2) - here)
        flux_down = face_down[pl.ds(first, rows)] * (here - pltpu.roll(here, 1, 2))
        behind = jnp.concatenate([flux_before, flux_x[:-1]], axis=0)
        write(first, rows, here + (flux_x - behind) + (flux_up - flux_down))
        return flux_x[-1:]

    lax.fori_loop(0, size_x // rows, step, jnp.zeros((1, GROUP, size_y), F32), unroll=4)


def on_grid(grid):
    def read(first, rows):
        return grid[pl.ds(first, rows)]

    def write(first, rows, value):
        grid[pl.ds(first, rows)] = value

    return read, write


def on_flat(flat, size_y):
    def at(x):
        return pl.ds(pl.multiple_of(x * size_y, size_y), size_y)

    def read(first, rows):
        return jnp.stack([flat[:, at(first + i)] for i in range(rows)], axis=0)

    def write(first, rows, value):
        for i in range(rows):
            flat[:, at(first + i)] = value[i]

    return read, write


def start_of(widths, j):
    return lax.fori_loop(0, j, lambda k, total: total + widths[k], jnp.int32(0))


def forward_kernel(size_x, size_y, groups, capacity, widths, control, diffusivity, diff_out, *rest):
    outs = rest[:PARTS]
    flat, one, two, *face_refs = rest[PARTS:]
    columns = size_x * size_y
    part = capacity // PARTS
    transpose_in(diffusivity, diff_out, size_x)
    faces(diff_out, *face_refs, size_x, size_y)
    transpose_in(control.at[0], one, size_x)
    stages = [on_grid((one, two)[i % 2]) for i in range(STEPS)] + [on_flat(flat, size_y)]
    for i in range(STEPS):
        sweep(stages[i][0], stages[i + 1][1], *face_refs, size_x, size_y)
    flat[:, columns:] = jnp.zeros((GROUP, flat.shape[1] - columns), F32)

    lane = lax.broadcasted_iota(jnp.int32, (GROUP, LANES), 1)
    tiles = part // LANES
    for j in range(groups):
        start = start_of(widths, j)
        base = start // LANES
        shift = start - base * LANES
        back = lax.rem(LANES - shift, LANES)
        low = lane < LANES - shift
        for c in range(PARTS):
            out = outs[c]
            begin = base + c * tiles

            def load(t):
                at = pl.multiple_of((begin + t) * LANES, LANES)
                return pltpu.roll(flat[:, pl.ds(at, LANES)], back, 1)

            now = load(0)
            for t in range(tiles):
                later = load(t + 1)
                out[j, :, t * LANES : (t + 1) * LANES] = jnp.where(low, now, later)
                now = later


def split2(value):
    high = value.astype(BF16)
    return high, (value - high.astype(F32)).astype(BF16)


def observation_kernel(part_rows, index, obs_cap, slots, rinv, out, split):
    step = pl.program_id(0)
    rows_here, levels = out.shape

    @pl.when(step == 0)
    def _():
        high, low = split2(rinv[0])
        split[:, :levels] = high
        split[:, levels:] = low

    core = lax.axis_index("mem") % 2
    first = index * part_rows + core * (part_rows // 2) + step * rows_here
    row = first + lax.broadcasted_iota(jnp.int32, (rows_here, obs_cap), 0)
    onehot = jnp.where(row == slots[...], 1.0, 0.0).astype(BF16)
    total = jnp.dot(onehot, split[...], preferred_element_type=F32)
    out[...] = total[:, :levels] + total[:, levels:]


def filter_kernel(core, vfilter, perturb, pieces, keep, send, table):
    levels = vfilter.shape[0]
    rows = keep.shape[0]
    step = pl.program_id(0)
    blocks = pl.num_programs(0) // 2

    @pl.when(step == 0)
    def _():
        high, low = split2(vfilter[...].T)
        table[:levels, :levels] = high
        table[levels:, :levels] = high
        table[:levels, levels:] = low
        table[levels:, levels:] = jnp.zeros_like(low)

    slab = pieces[...].reshape(levels, rows)
    both = jnp.concatenate(split2(slab.T), axis=1)
    products = jnp.dot(both, table[...], preferred_element_type=F32)
    result = perturb[0] * (products[:, :levels] + products[:, levels:])

    @pl.when(step < blocks)
    def _():
        keep[...] = result

    @pl.when(step >= blocks)
    def _():
        send[...] = result


def back_kernel(core, vfilter, perturb, adj_mine, adj_other, pieces, table):
    levels = vfilter.shape[0]
    step = pl.program_id(0)
    blocks = pl.num_programs(0) // 2

    @pl.when(step == 0)
    def _():
        high, low = split2(vfilter[...])
        table[:levels, :levels] = high
        table[levels:, :levels] = high
        table[:levels, levels:] = low
        table[levels:, levels:] = jnp.zeros_like(low)

    adj = jnp.where(step < blocks, adj_mine[...], adj_other[...])
    both = jnp.concatenate(split2(perturb[0] * adj), axis=1)
    products = jnp.dot(both, table[...], preferred_element_type=F32)
    result = (products[:, :levels] + products[:, levels:]).T
    pieces[...] = result.reshape(pieces.shape)


def backward_kernel(size_x, size_y, groups, capacity, widths, diff, *rest):
    ins = rest[:PARTS]
    out, staging, flat, one, two, *face_refs, sem = rest[PARTS:]
    part = capacity // PARTS
    level = pl.multiple_of(pl.program_id(0) * GROUP, GROUP)
    copies = [
        pltpu.make_async_copy(
            ins[c].at[:, pl.ds(level, GROUP), :], staging.at[:, :, pl.ds(c * part, part)], sem.at[c]
        )
        for c in range(PARTS)
    ]
    for copy in copies:
        copy.start()
    faces(diff, *face_refs, size_x, size_y)
    for copy in copies:
        copy.wait()

    lane = lax.broadcasted_iota(jnp.int32, (GROUP, LANES), 1)
    tiles = capacity // LANES

    def place(j, _):
        start = start_of(widths, j)
        base = start // LANES
        shift = start - base * LANES
        high = lane >= shift

        before = flat[:, pl.ds(pl.multiple_of(base * LANES, LANES), LANES)]
        for t in range(tiles):
            to = pl.multiple_of((base + t) * LANES, LANES)
            here = pltpu.roll(staging[j, :, t * LANES : (t + 1) * LANES], shift, 1)
            flat[:, pl.ds(to, LANES)] = jnp.where(high, here, before)
            before = here
        flat[:, pl.ds(pl.multiple_of((base + tiles) * LANES, LANES), LANES)] = before
        return 0

    lax.fori_loop(0, groups, place, 0)

    stages = [on_flat(flat, size_y)] + [on_grid((one, two)[i % 2]) for i in range(STEPS)]
    for i in range(STEPS):
        sweep(stages[i][0], stages[i + 1][1], *face_refs, size_x, size_y)
    grid = (one, two)[(STEPS - 1) % 2]

    def back(b, _):
        first = pl.multiple_of(b * 8, 8)
        out[0, :, pl.ds(first, 8), :] = jnp.swapaxes(grid[pl.ds(first, 8)], 0, 1)
        return 0

    lax.fori_loop(0, size_x // 8, back, 0, unroll=2)


def after(value, *others):
    return lax.optimization_barrier((value,) + others)[0]


def body(control, diffusivity, perturb, vertical_filter, sub_widths, obs_raw, obs_counts, obs_rinv):
    members, levels_here, size_x, size_y = control.shape
    columns = size_x * size_y
    capacity = perturb.shape[1]
    levels = perturb.shape[2]
    groups = sub_widths.shape[0]
    obs_cap = obs_raw.shape[1]
    part = capacity // PARTS
    half = part // 2
    n_mem = lax.axis_size("mem")
    me = lax.axis_index("lev")
    smem = pl.BlockSpec(memory_space=pltpu.SMEM)
    params = pltpu.CompilerParams(vmem_limit_bytes=56 << 20)
    flat_width = columns + capacity + LANES
    pieces_shape = jax.ShapeDtypeStruct((groups, levels_here, part), F32)
    steps = levels_here // GROUP

    results = pl.pallas_call(
        functools.partial(forward_kernel, size_x, size_y, groups, capacity),
        grid=(steps,),
        in_specs=[
            smem,
            pl.BlockSpec((1, GROUP, size_x, size_y), lambda g: (0, g, 0, 0)),
            pl.BlockSpec((GROUP, size_x, size_y), lambda g: (g, 0, 0)),
        ],
        out_specs=[pl.BlockSpec((size_x, GROUP, size_y), lambda g: (0, g, 0))]
        + [pl.BlockSpec((groups, GROUP, part), lambda g: (0, g, 0))] * PARTS,
        out_shape=[jax.ShapeDtypeStruct((size_x, levels_here, size_y), F32)] + [pieces_shape] * PARTS,
        scratch_shapes=[
            pltpu.VMEM((GROUP, flat_width), F32),
        ]
        + [pltpu.VMEM((size_x, GROUP, size_y), F32)] * 5,
        compiler_params=params,
        name="smooth_and_cut",
    )(sub_widths, control, diffusivity)
    diff = results[0]
    outgoing = results[1:]

    width = sub_widths[me]
    live = jnp.arange(obs_cap, dtype=jnp.int32) < obs_counts[me]
    slots = jnp.where(live, obs_raw[0] % width, -1)[None, :]

    vfilter = vertical_filter
    width = half
    blocks = part // width
    some = blocks // 2

    def block_of(g, core):
        return (g // some + core[0]) % 2 * some + g % some

    square = pl.BlockSpec((levels, levels), lambda g, core: (0, 0))
    slab = pl.BlockSpec((groups, levels_here, width), lambda g, core: (0, 0, block_of(g, core)))
    first_half = pl.BlockSpec((width, levels), lambda g, core: (jnp.minimum(g, some - 1), 0))
    second_half = pl.BlockSpec((width, levels), lambda g, core: (jnp.maximum(g - some, 0), 0))
    half_shape = jax.ShapeDtypeStruct((half, levels), F32)
    core = (lax.axis_index("mem") % 2).astype(jnp.int32)[None]
    table = pltpu.VMEM((2 * levels, 2 * levels), BF16)
    cost = pl.CostEstimate(flops=0, bytes_accessed=0, transcendentals=0)
    rows_here = 256

    def weights(c, slots):
        return pl.pallas_call(
            functools.partial(observation_kernel, part, c, obs_cap),
            grid=(half // rows_here,),
            in_specs=[
                pl.BlockSpec((1, obs_cap), lambda g: (0, 0)),
                pl.BlockSpec((1, obs_cap, levels), lambda g: (0, 0, 0)),
            ],
            out_specs=pl.BlockSpec((rows_here, levels), lambda g: (g, 0)),
            out_shape=jax.ShapeDtypeStruct((half, levels), F32),
            scratch_shapes=[pltpu.VMEM((obs_cap, 2 * levels), BF16)],
            compiler_params=params,
            cost_estimate=cost,
            name="observation_weights",
        )(slots, obs_rinv)

    def perturb_part(c):
        return pl.BlockSpec((1, width, levels), lambda g, core: (0, c * blocks + block_of(g, core), 0))

    def filter_forward(c, vfilter, pieces):
        return pl.pallas_call(
            filter_kernel,
            grid_spec=pltpu.PrefetchScalarGridSpec(
                num_scalar_prefetch=1,
                grid=(blocks,),
                in_specs=[square, perturb_part(c), slab],
                out_specs=[first_half, second_half],
                scratch_shapes=[table],
            ),
            out_shape=[half_shape, half_shape],
            compiler_params=params,
            cost_estimate=cost,
            name="filter_forward",
        )(core, vfilter, perturb, pieces)

    def filter_backward(c, adj_mine, adj_other):
        return pl.pallas_call(
            back_kernel,
            grid_spec=pltpu.PrefetchScalarGridSpec(
                num_scalar_prefetch=1,
                grid=(blocks,),
                in_specs=[square, perturb_part(c), first_half, second_half],
                out_specs=slab,
                scratch_shapes=[table],
            ),
            out_shape=pieces_shape,
            compiler_params=params,
            cost_estimate=cost,
            name="filter_backward",
        )(core, vfilter, perturb, adj_mine, adj_other)

    def exchange(pieces):
        return lax.all_to_all(pieces, "lev", 0, 0, tiled=True)

    def sum_members(keep, send):
        total = keep + lax.ppermute(send, "mem", flip_pairs(n_mem, 1))
        bit = 2
        while bit < n_mem:
            total = total + lax.ppermute(total, "mem", flip_pairs(n_mem, bit))
            bit *= 2
        return total

    def adjoint(total, obs_weight):
        mine = total * obs_weight
        return mine, lax.ppermute(mine, "mem", flip_pairs(n_mem, 1))

    got = [exchange(outgoing[c]) for c in range(PARTS)]
    weight = [weights(c, slots) for c in range(PARTS)]
    back = []
    gate_filter = []
    for c in range(PARTS):
        gated = after(vfilter, *gate_filter) if gate_filter else vfilter
        keep, send = filter_forward(c, gated, got[c])
        mine, other = adjoint(sum_members(keep, send), weight[c])
        adjoint_pieces = filter_backward(c, mine, other)
        pieces = exchange(adjoint_pieces)
        gate_filter = [adjoint_pieces]
        back.append(pieces)

    return pl.pallas_call(
        functools.partial(backward_kernel, size_x, size_y, groups, capacity),
        grid=(steps,),
        in_specs=[
            smem,
            pl.BlockSpec((size_x, GROUP, size_y), lambda g: (0, g, 0)),
        ]
        + [pl.BlockSpec(memory_space=pl.ANY)] * PARTS,
        out_specs=pl.BlockSpec((1, GROUP, size_x, size_y), lambda g: (0, g, 0, 0)),
        out_shape=jax.ShapeDtypeStruct((members, levels_here, size_x, size_y), F32),
        scratch_shapes=[
            pltpu.VMEM((groups, GROUP, capacity), F32),
            pltpu.VMEM((GROUP, flat_width), F32),
        ]
        + [pltpu.VMEM((size_x, GROUP, size_y), F32)] * 5
        + [pltpu.SemaphoreType.DMA((PARTS,))],
        compiler_params=params,
        name="place_and_smooth",
    )(sub_widths, diff, *back)


def solution(mesh):
    return jax.shard_map(
        body,
        mesh=mesh,
        in_specs=(
            P("mem", "lev", None, None),
            P("lev", None, None),
            P("mem", "lev", None),
            P(),
            P(),
            P("lev", None),
            P(),
            P("lev", None, None),
        ),
        out_specs=P("mem", "lev", None, None),
        check_vma=False,
    )
```

```python
import functools

import jax
import jax.numpy as jnp
from jax import lax
from jax.experimental import pallas as pl
from jax.experimental.pallas import tpu as pltpu
from jax.sharding import PartitionSpec as P

STEPS = 4
PARTS = 2
LANES = 128
GROUP = 8
F32 = jnp.float32
BF16 = jnp.bfloat16


def flip_pairs(size, bit):
    return [(i, i ^ bit) for i in range(size)]


def transpose_in(src, dst, size_x):
    def step(b, _):
        first = pl.multiple_of(b * 8, 8)
        dst[pl.ds(first, 8)] = jnp.swapaxes(src[:, pl.ds(first, 8), :], 0, 1)
        return 0

    lax.fori_loop(0, size_x // 8, step, 0, unroll=2)


def faces(diff, face_x, face_up, face_down, size_x, size_y):
    lane = lax.broadcasted_iota(jnp.int32, (1, GROUP, size_y), 2)
    rows = 16

    def step(b, _):
        first = pl.multiple_of(b * rows, rows)
        here = diff[pl.ds(first, rows)]
        beyond = diff[pl.ds(jnp.minimum(first + rows, size_x - 1), 1)]
        ahead = jnp.concatenate([here[1:], beyond], axis=0)
        row = first + lax.broadcasted_iota(jnp.int32, (rows, GROUP, size_y), 0)
        face_x[pl.ds(first, rows)] = jnp.where(row < size_x - 1, 0.5 * (here + ahead), 0.0)
        up = 0.5 * (here + pltpu.roll(here, size_y - 1, 2))
        face_up[pl.ds(first, rows)] = jnp.where(lane < size_y - 1, up, 0.0)
        down = 0.5 * (here + pltpu.roll(here, 1, 2))
        face_down[pl.ds(first, rows)] = jnp.where(lane > 0, down, 0.0)
        return 0

    lax.fori_loop(0, size_x // rows, step, 0)


def sweep(read, write, face_x, face_up, face_down, size_x, size_y):
    rows = 8

    def step(b, flux_before):
        first = pl.multiple_of(b * rows, rows)
        here = read(first, rows)
        beyond = read(jnp.minimum(first + rows, size_x - 1), 1)
        ahead = jnp.concatenate([here[1:], beyond], axis=0)
        flux_x = face_x[pl.ds(first, rows)] * (ahead - here)
        flux_up = face_up[pl.ds(first, rows)] * (pltpu.roll(here, size_y - 1, 2) - here)
        flux_down = face_down[pl.ds(first, rows)] * (here - pltpu.roll(here, 1, 2))
        behind = jnp.concatenate([flux_before, flux_x[:-1]], axis=0)
        write(first, rows, here + (flux_x - behind) + (flux_up - flux_down))
        return flux_x[-1:]

    lax.fori_loop(0, size_x // rows, step, jnp.zeros((1, GROUP, size_y), F32), unroll=4)


def on_grid(grid):
    def read(first, rows):
        return grid[pl.ds(first, rows)]

    def write(first, rows, value):
        grid[pl.ds(first, rows)] = value

    return read, write


def on_flat(flat, size_y):
    def at(x):
        return pl.ds(pl.multiple_of(x * size_y, size_y), size_y)

    def read(first, rows):
        return jnp.stack([flat[:, at(first + i)] for i in range(rows)], axis=0)

    def write(first, rows, value):
        for i in range(rows):
            flat[:, at(first + i)] = value[i]

    return read, write


def start_of(widths, j):
    return lax.fori_loop(0, j, lambda k, total: total + widths[k], jnp.int32(0))


def turns_of(groups):
    return [0] + list(range(groups // 2, groups)) + list(range(groups // 2 - 1, 0, -1))


def forward_kernel(size_x, size_y, groups, widths, control, diffusivity, *rest):
    *rest, flat, one, two, face_x, face_up, face_down = rest
    diff_out, later, *sooner = rest[-groups - 2 :]
    face_refs = (face_x, face_up, face_down)
    columns = size_x * size_y
    part = later.shape[2]
    transpose_in(diffusivity, diff_out, size_x)
    faces(diff_out, *face_refs, size_x, size_y)
    transpose_in(control.at[0], one, size_x)
    stages = [on_grid((one, two)[i % 2]) for i in range(STEPS)] + [on_flat(flat, size_y)]
    for i in range(STEPS):
        sweep(stages[i][0], stages[i + 1][1], *face_refs, size_x, size_y)
    flat[:, columns:] = jnp.zeros((GROUP, flat.shape[1] - columns), F32)

    lane = lax.broadcasted_iota(jnp.int32, (GROUP, LANES), 1)
    me = lax.axis_index("lev")
    tiles = part // LANES

    def cut(j, c, store):
        start = start_of(widths, j)
        base = start // LANES
        shift = start - base * LANES
        back = lax.rem(LANES - shift, LANES)
        low = lane < LANES - shift
        begin = base + c * tiles

        def load(t):
            at = pl.multiple_of((begin + t) * LANES, LANES)
            return pltpu.roll(flat[:, pl.ds(at, LANES)], back, 1)

        now = load(0)
        for t in range(tiles):
            following = load(t + 1)
            store(t, jnp.where(low, now, following))
            now = following

    for d, turn in enumerate(turns_of(groups)):

        def store_sooner(t, value):
            sooner[d][:, t * LANES : (t + 1) * LANES] = value

        def store_later(t, value):
            later[d, :, t * LANES : (t + 1) * LANES] = value

        cut(jnp.bitwise_xor(me, turn), 0, store_sooner)
        cut(d, 1, store_later)


def split2(value):
    high = value.astype(BF16)
    return high, (value - high.astype(F32)).astype(BF16)


def observation_kernel(part_rows, index, obs_cap, slots, rinv, out, split):
    step = pl.program_id(0)
    rows_here, levels = out.shape

    @pl.when(step == 0)
    def _():
        high, low = split2(rinv[0])
        split[:, :levels] = high
        split[:, levels:] = low

    core = lax.axis_index("mem") % 2
    first = index * part_rows + core * (part_rows // 2) + step * rows_here
    row = first + lax.broadcasted_iota(jnp.int32, (rows_here, obs_cap), 0)
    onehot = jnp.where(row == slots[...], 1.0, 0.0).astype(BF16)
    total = jnp.dot(onehot, split[...], preferred_element_type=F32)
    out[...] = total[:, :levels] + total[:, levels:]


def filter_kernel(core, vfilter, perturb, *rest):
    *pieces, keep, send, table = rest
    levels = vfilter.shape[0]
    rows = keep.shape[0]
    step = pl.program_id(0)
    blocks = pl.num_programs(0) // 2

    @pl.when(step == 0)
    def _():
        high, low = split2(vfilter[...].T)
        table[:levels, :levels] = high
        table[levels:, :levels] = high
        table[:levels, levels:] = low
        table[levels:, levels:] = jnp.zeros_like(low)

    slab = jnp.concatenate([piece[...].reshape(-1, rows) for piece in pieces], axis=0)
    both = jnp.concatenate(split2(slab.T), axis=1)
    products = jnp.dot(both, table[...], preferred_element_type=F32)
    result = perturb[0] * (products[:, :levels] + products[:, levels:])

    @pl.when(step < blocks)
    def _():
        keep[...] = result

    @pl.when(step >= blocks)
    def _():
        send[...] = result


def back_kernel(core, vfilter, perturb, adj_mine, adj_other, *rest):
    *pieces, table = rest
    levels = vfilter.shape[0]
    step = pl.program_id(0)
    blocks = pl.num_programs(0) // 2

    @pl.when(step == 0)
    def _():
        high, low = split2(vfilter[...])
        table[:levels, :levels] = high
        table[levels:, :levels] = high
        table[:levels, levels:] = low
        table[levels:, levels:] = jnp.zeros_like(low)

    adj = jnp.where(step < blocks, adj_mine[...], adj_other[...])
    both = jnp.concatenate(split2(perturb[0] * adj), axis=1)
    products = jnp.dot(both, table[...], preferred_element_type=F32)
    result = (products[:, :levels] + products[:, levels:]).T
    first = 0
    for piece in pieces:
        count = piece.size // piece.shape[-1]
        piece[...] = result[first : first + count].reshape(piece.shape)
        first += count


def backward_kernel(size_x, size_y, groups, capacity, group, widths, diff, *rest):
    *rest, staging, flat, one, two, face_x, face_up, face_down, sem = rest
    face_refs = (face_x, face_up, face_down)
    sooner, *later = rest[: groups + 1]
    out = rest[-1]
    part = capacity // PARTS
    me = lax.axis_index("lev")
    copies = [
        pltpu.make_async_copy(
            sooner.at[:, pl.ds(group * GROUP, GROUP), :], staging.at[:, :, pl.ds(0, part)], sem.at[0]
        )
    ]
    for d, turn in enumerate(turns_of(groups)):
        copies.append(
            pltpu.make_async_copy(
                later[d], staging.at[jnp.bitwise_xor(me, turn), :, pl.ds(part, part)], sem.at[1 + d]
            )
        )
    for copy in copies:
        copy.start()
    faces(diff, *face_refs, size_x, size_y)
    for copy in copies:
        copy.wait()

    lane = lax.broadcasted_iota(jnp.int32, (GROUP, LANES), 1)
    tiles = capacity // LANES

    def place(j, _):
        start = start_of(widths, j)
        base = start // LANES
        shift = start - base * LANES
        high = lane >= shift

        before = flat[:, pl.ds(pl.multiple_of(base * LANES, LANES), LANES)]
        for t in range(tiles):
            to = pl.multiple_of((base + t) * LANES, LANES)
            here = pltpu.roll(staging[j, :, t * LANES : (t + 1) * LANES], shift, 1)
            flat[:, pl.ds(to, LANES)] = jnp.where(high, here, before)
            before = here
        flat[:, pl.ds(pl.multiple_of((base + tiles) * LANES, LANES), LANES)] = before
        return 0

    lax.fori_loop(0, groups, place, 0)

    stages = [on_flat(flat, size_y)] + [on_grid((one, two)[i % 2]) for i in range(STEPS)]
    for i in range(STEPS):
        sweep(stages[i][0], stages[i + 1][1], *face_refs, size_x, size_y)
    grid = (one, two)[(STEPS - 1) % 2]

    def back(b, _):
        first = pl.multiple_of(b * 8, 8)
        out[0, :, pl.ds(first, 8), :] = jnp.swapaxes(grid[pl.ds(first, 8)], 0, 1)
        return 0

    lax.fori_loop(0, size_x // 8, back, 0, unroll=2)


def after(value, *others):
    return lax.optimization_barrier((value,) + others)[0]


def body(control, diffusivity, perturb, vertical_filter, sub_widths, obs_raw, obs_counts, obs_rinv):
    members, levels_here, size_x, size_y = control.shape
    columns = size_x * size_y
    capacity = perturb.shape[1]
    levels = perturb.shape[2]
    groups = sub_widths.shape[0]
    obs_cap = obs_raw.shape[1]
    part = capacity // PARTS
    half = part // 2
    n_mem = lax.axis_size("mem")
    me = lax.axis_index("lev")
    smem = pl.BlockSpec(memory_space=pltpu.SMEM)
    params = pltpu.CompilerParams(vmem_limit_bytes=56 << 20)
    flat_width = columns + capacity + LANES
    piece_shape = jax.ShapeDtypeStruct((GROUP, part), F32)
    pieces_shape = jax.ShapeDtypeStruct((groups, levels_here, part), F32)
    n_groups = levels_here // GROUP
    any_spec = pl.BlockSpec(memory_space=pl.ANY)
    turns = turns_of(groups)

    def permute(piece, d):
        return lax.ppermute(piece, "lev", flip_pairs(groups, turns[d])) if d else piece

    diffs, later, got = [], None, {}
    widths = sub_widths
    for group in range(n_groups):
        before = [] if later is None else [later]
        results = pl.pallas_call(
            functools.partial(forward_kernel, size_x, size_y, groups),
            grid=(1,),
            in_specs=[
                smem,
                pl.BlockSpec((1, GROUP, size_x, size_y), lambda g, group=group: (0, group, 0, 0)),
                pl.BlockSpec((GROUP, size_x, size_y), lambda g, group=group: (group, 0, 0)),
            ]
            + [any_spec] * len(before),
            out_specs=[
                pl.BlockSpec((size_x, GROUP, size_y), lambda g: (0, 0, 0)),
                pl.BlockSpec((groups, GROUP, part), lambda g, group=group: (0, group, 0)),
            ]
            + [pl.BlockSpec((GROUP, part), lambda g: (0, 0))] * groups,
            out_shape=[jax.ShapeDtypeStruct((size_x, GROUP, size_y), F32), pieces_shape] + [piece_shape] * groups,
            input_output_aliases={3: 1} if before else {},
            scratch_shapes=[pltpu.VMEM((GROUP, flat_width), F32)]
            + [pltpu.VMEM((size_x, GROUP, size_y), F32)] * 5,
            compiler_params=params,
            cost_estimate=pl.CostEstimate(flops=0, bytes_accessed=0, transcendentals=0),
            name="smooth_and_cut",
        )(widths, control, diffusivity, *before)
        diffs.append(results[0])
        later = results[1]
        for d in range(groups):
            got[d, group] = permute(results[2 + d], d)
        widths = after(sub_widths, got[7, group])

    width = sub_widths[me]
    live = jnp.arange(obs_cap, dtype=jnp.int32) < obs_counts[me]
    slots = jnp.where(live, obs_raw[0] % width, -1)[None, :]

    order = jnp.bitwise_xor(me, jnp.array(turns, jnp.int32))
    turned = vertical_filter.reshape(levels, groups, levels_here)[:, order, :].reshape(levels, levels)

    width = half
    blocks = part // width
    some = blocks // 2

    def block_of(g, core):
        return (g // some + core[0]) % 2 * some + g % some

    square = pl.BlockSpec((levels, levels), lambda g, core: (0, 0))
    slab = pl.BlockSpec((groups, levels_here, width), lambda g, core: (0, 0, block_of(g, core)))
    strip = pl.BlockSpec((GROUP, width), lambda g, core: (0, block_of(g, core)))
    n_strips = groups * n_groups
    first_half = pl.BlockSpec((width, levels), lambda g, core: (jnp.minimum(g, some - 1), 0))
    second_half = pl.BlockSpec((width, levels), lambda g, core: (jnp.maximum(g - some, 0), 0))
    half_shape = jax.ShapeDtypeStruct((half, levels), F32)
    core = (lax.axis_index("mem") % 2).astype(jnp.int32)[None]
    table = pltpu.VMEM((2 * levels, 2 * levels), BF16)
    cost = pl.CostEstimate(flops=0, bytes_accessed=0, transcendentals=0)
    rows_here = 256

    def weights(c, slots):
        return pl.pallas_call(
            functools.partial(observation_kernel, part, c, obs_cap),
            grid=(half // rows_here,),
            in_specs=[
                pl.BlockSpec((1, obs_cap), lambda g: (0, 0)),
                pl.BlockSpec((1, obs_cap, levels), lambda g: (0, 0, 0)),
            ],
            out_specs=pl.BlockSpec((rows_here, levels), lambda g: (g, 0)),
            out_shape=jax.ShapeDtypeStruct((half, levels), F32),
            scratch_shapes=[pltpu.VMEM((obs_cap, 2 * levels), BF16)],
            compiler_params=params,
            cost_estimate=cost,
            name="observation_weights",
        )(slots, obs_rinv)

    def perturb_part(c):
        return pl.BlockSpec((1, width, levels), lambda g, core: (0, c * blocks + block_of(g, core), 0))

    def filter_forward(c, vfilter, *pieces):
        return pl.pallas_call(
            filter_kernel,
            grid_spec=pltpu.PrefetchScalarGridSpec(
                num_scalar_prefetch=1,
                grid=(blocks,),
                in_specs=[square, perturb_part(c)] + ([slab] if len(pieces) == 1 else [strip] * n_strips),
                out_specs=[first_half, second_half],
                scratch_shapes=[table],
            ),
            out_shape=[half_shape, half_shape],
            compiler_params=params,
            cost_estimate=cost,
            name="filter_forward",
        )(core, vfilter, perturb, *pieces)

    def filter_backward(c, vfilter, adj_mine, adj_other, strips):
        return pl.pallas_call(
            back_kernel,
            grid_spec=pltpu.PrefetchScalarGridSpec(
                num_scalar_prefetch=1,
                grid=(blocks,),
                in_specs=[square, perturb_part(c), first_half, second_half],
                out_specs=[strip] * n_strips if strips else [slab],
                scratch_shapes=[table],
            ),
            out_shape=[piece_shape] * n_strips if strips else [pieces_shape],
            compiler_params=params,
            cost_estimate=cost,
            name="filter_backward",
        )(core, vfilter, perturb, adj_mine, adj_other)

    def exchange(pieces):
        return lax.all_to_all(pieces, "lev", 0, 0, tiled=True)

    def sum_members(keep, send):
        total = keep + lax.ppermute(send, "mem", flip_pairs(n_mem, 1))
        bit = 2
        while bit < n_mem:
            total = total + lax.ppermute(total, "mem", flip_pairs(n_mem, bit))
            bit *= 2
        return total

    def adjoint(total, obs_weight):
        mine = total * obs_weight
        return mine, lax.ppermute(mine, "mem", flip_pairs(n_mem, 1))

    in_order = [(d, group) for d in range(groups) for group in range(n_groups)]
    slots = after(slots, got[1, 0])
    weight = [weights(c, slots) for c in range(PARTS)]
    got_later = exchange(later)

    keep, send = filter_forward(0, turned, *[got[key] for key in in_order])
    mine, other = adjoint(sum_members(keep, send), weight[0])
    pieces = filter_backward(0, vertical_filter, mine, other, False)[0]
    back_sooner = exchange(pieces)

    keep, send = filter_forward(1, after(vertical_filter, pieces), got_later)
    mine, other = adjoint(sum_members(keep, send), weight[1])
    pieces = filter_backward(1, turned, mine, other, True)
    out = None
    for group in range(n_groups):
        before = [] if out is None else [out]
        back = []
        for d in range(groups):
            piece = pieces[in_order.index((d, group))]
            back.append(permute(after(piece, out) if before and d in (6,) else piece, d))
        out = pl.pallas_call(
            functools.partial(backward_kernel, size_x, size_y, groups, capacity, group),
            grid=(1,),
            in_specs=[smem, pl.BlockSpec((size_x, GROUP, size_y), lambda g: (0, 0, 0))]
            + [any_spec] * (1 + groups + len(before)),
            out_specs=pl.BlockSpec((1, GROUP, size_x, size_y), lambda g, group=group: (0, group, 0, 0)),
            out_shape=jax.ShapeDtypeStruct((members, levels_here, size_x, size_y), F32),
            input_output_aliases={3 + groups: 0} if before else {},
            scratch_shapes=[
                pltpu.VMEM((groups, GROUP, capacity), F32),
                pltpu.VMEM((GROUP, flat_width), F32),
            ]
            + [pltpu.VMEM((size_x, GROUP, size_y), F32)] * 5
            + [pltpu.SemaphoreType.DMA((1 + groups,))],
            compiler_params=params,
            cost_estimate=pl.CostEstimate(flops=0, bytes_accessed=0, transcendentals=0),
            name="place_and_smooth",
        )(sub_widths, diffs[group], back_sooner, *back, *before)
    return out


def solution(mesh):
    return jax.shard_map(
        body,
        mesh=mesh,
        in_specs=(
            P("mem", "lev", None, None),
            P("lev", None, None),
            P("mem", "lev", None),
            P(),
            P(),
            P("lev", None),
            P(),
            P("lev", None, None),
        ),
        out_specs=P("mem", "lev", None, None),
        check_vma=False,
    )
```

```python
import functools

import jax
import jax.numpy as jnp
from jax import lax
from jax.experimental import pallas as pl
from jax.experimental.pallas import tpu as pltpu
from jax.sharding import PartitionSpec as P

STEPS = 4
PARTS = 2
LANES = 128
GROUP = 8
F32 = jnp.float32
BF16 = jnp.bfloat16


def flip_pairs(size, bit):
    return [(i, i ^ bit) for i in range(size)]


def transpose_in(src, dst, size_x):
    def step(b, _):
        first = pl.multiple_of(b * 8, 8)
        dst[pl.ds(first, 8)] = jnp.swapaxes(src[:, pl.ds(first, 8), :], 0, 1)
        return 0

    lax.fori_loop(0, size_x // 8, step, 0, unroll=2)


def faces(diff, face_x, face_up, face_down, size_x, size_y):
    lane = lax.broadcasted_iota(jnp.int32, (1, GROUP, size_y), 2)
    rows = 16

    def step(b, _):
        first = pl.multiple_of(b * rows, rows)
        here = diff[pl.ds(first, rows)]
        beyond = diff[pl.ds(jnp.minimum(first + rows, size_x - 1), 1)]
        ahead = jnp.concatenate([here[1:], beyond], axis=0)
        row = first + lax.broadcasted_iota(jnp.int32, (rows, GROUP, size_y), 0)
        face_x[pl.ds(first, rows)] = jnp.where(row < size_x - 1, 0.5 * (here + ahead), 0.0)
        up = 0.5 * (here + pltpu.roll(here, size_y - 1, 2))
        face_up[pl.ds(first, rows)] = jnp.where(lane < size_y - 1, up, 0.0)
        down = 0.5 * (here + pltpu.roll(here, 1, 2))
        face_down[pl.ds(first, rows)] = jnp.where(lane > 0, down, 0.0)
        return 0

    lax.fori_loop(0, size_x // rows, step, 0)


def sweep(read, write, face_x, face_up, face_down, size_x, size_y):
    rows = 8

    def step(b, flux_before):
        first = pl.multiple_of(b * rows, rows)
        here = read(first, rows)
        beyond = read(jnp.minimum(first + rows, size_x - 1), 1)
        ahead = jnp.concatenate([here[1:], beyond], axis=0)
        flux_x = face_x[pl.ds(first, rows)] * (ahead - here)
        flux_up = face_up[pl.ds(first, rows)] * (pltpu.roll(here, size_y - 1, 2) - here)
        flux_down = face_down[pl.ds(first, rows)] * (here - pltpu.roll(here, 1, 2))
        behind = jnp.concatenate([flux_before, flux_x[:-1]], axis=0)
        write(first, rows, here + (flux_x - behind) + (flux_up - flux_down))
        return flux_x[-1:]

    lax.fori_loop(0, size_x // rows, step, jnp.zeros((1, GROUP, size_y), F32), unroll=4)


def on_grid(grid):
    def read(first, rows):
        return grid[pl.ds(first, rows)]

    def write(first, rows, value):
        grid[pl.ds(first, rows)] = value

    return read, write


def on_flat(flat, size_y):
    def at(x):
        return pl.ds(pl.multiple_of(x * size_y, size_y), size_y)

    def read(first, rows):
        return jnp.stack([flat[:, at(first + i)] for i in range(rows)], axis=0)

    def write(first, rows, value):
        for i in range(rows):
            flat[:, at(first + i)] = value[i]

    return read, write


def start_of(widths, j):
    return lax.fori_loop(0, j, lambda k, total: total + widths[k], jnp.int32(0))


def turns_in(groups):
    return list(range(groups))


def turns_out(groups, last):
    near, far = list(range(groups // 2 - 1, 1, -1)), list(range(groups // 2, groups))
    return [0, 1] + far + near if last else [0] + far + near + [1]


def forward_kernel(size_x, size_y, groups, n_sooner, widths, control, diffusivity, *rest):
    *rest, flat, one, two, face_x, face_up, face_down = rest
    diff_out, later, *sooner = rest[-n_sooner - 2 :]
    face_refs = (face_x, face_up, face_down)
    columns = size_x * size_y
    part = later.shape[2]
    transpose_in(diffusivity, diff_out, size_x)
    faces(diff_out, *face_refs, size_x, size_y)
    transpose_in(control.at[0], one, size_x)
    stages = [on_grid((one, two)[i % 2]) for i in range(STEPS)] + [on_flat(flat, size_y)]
    for i in range(STEPS):
        sweep(stages[i][0], stages[i + 1][1], *face_refs, size_x, size_y)
    flat[:, columns:] = jnp.zeros((GROUP, flat.shape[1] - columns), F32)

    lane = lax.broadcasted_iota(jnp.int32, (GROUP, LANES), 1)
    me = lax.axis_index("lev")
    tiles = part // LANES

    def cut(j, c, store):
        start = start_of(widths, j)
        base = start // LANES
        shift = start - base * LANES
        back = lax.rem(LANES - shift, LANES)
        low = lane < LANES - shift
        begin = base + c * tiles

        def load(t):
            at = pl.multiple_of((begin + t) * LANES, LANES)
            return pltpu.roll(flat[:, pl.ds(at, LANES)], back, 1)

        now = load(0)
        for t in range(tiles):
            following = load(t + 1)
            store(t, jnp.where(low, now, following))
            now = following

    for d, turn in enumerate(turns_in(groups)):

        def store_sooner(t, value):
            target = sooner[d] if n_sooner == groups else sooner[0].at[d]
            target[:, t * LANES : (t + 1) * LANES] = value

        def store_later(t, value):
            later[d, :, t * LANES : (t + 1) * LANES] = value

        cut(jnp.bitwise_xor(me, turn) if n_sooner == groups else d, 0, store_sooner)
        cut(d, 1, store_later)


def split2(value):
    high = value.astype(BF16)
    return high, (value - high.astype(F32)).astype(BF16)


def observation_kernel(part_rows, index, obs_cap, slots, rinv, out, split):
    step = pl.program_id(0)
    rows_here, levels = out.shape

    @pl.when(step == 0)
    def _():
        high, low = split2(rinv[0])
        split[:, :levels] = high
        split[:, levels:] = low

    core = lax.axis_index("mem") % 2
    first = index * part_rows + core * (part_rows // 2) + step * rows_here
    row = first + lax.broadcasted_iota(jnp.int32, (rows_here, obs_cap), 0)
    onehot = jnp.where(row == slots[...], 1.0, 0.0).astype(BF16)
    total = jnp.dot(onehot, split[...], preferred_element_type=F32)
    out[...] = total[:, :levels] + total[:, levels:]


def filter_kernel(core, vfilter, perturb, *rest):
    *pieces, keep, send, table = rest
    levels = vfilter.shape[0]
    rows = keep.shape[0]
    step = pl.program_id(0)
    blocks = pl.num_programs(0) // 2

    @pl.when(step == 0)
    def _():
        high, low = split2(vfilter[...].T)
        table[:levels, :levels] = high
        table[levels:, :levels] = high
        table[:levels, levels:] = low
        table[levels:, levels:] = jnp.zeros_like(low)

    slab = jnp.concatenate([piece[...].reshape(-1, rows) for piece in pieces], axis=0)
    both = jnp.concatenate(split2(slab.T), axis=1)
    products = jnp.dot(both, table[...], preferred_element_type=F32)
    result = perturb[0] * (products[:, :levels] + products[:, levels:])

    @pl.when(step < blocks)
    def _():
        keep[...] = result

    @pl.when(step >= blocks)
    def _():
        send[...] = result


def back_kernel(n_adj, core, vfilter, perturb, *rest):
    adj_mine, adj_other = rest[:n_adj], rest[n_adj : 2 * n_adj]
    *pieces, table = rest[2 * n_adj :]
    levels = vfilter.shape[0]
    step = pl.program_id(0)
    blocks = pl.num_programs(0) // 2

    @pl.when(step == 0)
    def _():
        high, low = split2(vfilter[...])
        table[:levels, :levels] = high
        table[levels:, :levels] = high
        table[:levels, levels:] = low
        table[levels:, levels:] = jnp.zeros_like(low)

    adj = jnp.concatenate([jnp.where(step < blocks, a[...], b[...]) for a, b in zip(adj_mine, adj_other)], axis=0)
    both = jnp.concatenate(split2(perturb[0] * adj), axis=1)
    products = jnp.dot(both, table[...], preferred_element_type=F32)
    result = (products[:, :levels] + products[:, levels:]).T
    first = 0
    for piece in pieces:
        count = piece.size // piece.shape[-1]
        piece[...] = result[first : first + count].reshape(piece.shape)
        first += count


def backward_kernel(size_x, size_y, groups, capacity, group, last, widths, diff, *rest):
    *rest, staging, flat, one, two, face_x, face_up, face_down, sem = rest
    face_refs = (face_x, face_up, face_down)
    sooner, *later = rest[: groups + 1]
    out = rest[-1]
    part = capacity // PARTS
    me = lax.axis_index("lev")
    copies = [
        pltpu.make_async_copy(
            sooner.at[:, pl.ds(group * GROUP, GROUP), :], staging.at[:, :, pl.ds(0, part)], sem.at[0]
        )
    ]
    late = pl.ds(part, part)
    targets = [staging.at[jnp.bitwise_xor(me, turn), :, late] for turn in turns_out(groups, last)]
    for d in range(groups):
        copies.append(pltpu.make_async_copy(later[d], targets[d], sem.at[1 + d]))
    for copy in copies:
        copy.start()
    faces(diff, *face_refs, size_x, size_y)
    for copy in copies:
        copy.wait()

    lane = lax.broadcasted_iota(jnp.int32, (GROUP, LANES), 1)
    tiles = capacity // LANES

    def place(j, _):
        start = start_of(widths, j)
        base = start // LANES
        shift = start - base * LANES
        high = lane >= shift

        before = flat[:, pl.ds(pl.multiple_of(base * LANES, LANES), LANES)]
        for t in range(tiles):
            to = pl.multiple_of((base + t) * LANES, LANES)
            here = pltpu.roll(staging[j, :, t * LANES : (t + 1) * LANES], shift, 1)
            flat[:, pl.ds(to, LANES)] = jnp.where(high, here, before)
            before = here
        flat[:, pl.ds(pl.multiple_of((base + tiles) * LANES, LANES), LANES)] = before
        return 0

    lax.fori_loop(0, groups, place, 0)

    stages = [on_flat(flat, size_y)] + [on_grid((one, two)[i % 2]) for i in range(STEPS)]
    for i in range(STEPS):
        sweep(stages[i][0], stages[i + 1][1], *face_refs, size_x, size_y)
    grid = (one, two)[(STEPS - 1) % 2]

    def back(b, _):
        first = pl.multiple_of(b * 8, 8)
        out[0, :, pl.ds(first, 8), :] = jnp.swapaxes(grid[pl.ds(first, 8)], 0, 1)
        return 0

    lax.fori_loop(0, size_x // 8, back, 0, unroll=2)


def after(value, *others):
    return lax.optimization_barrier((value,) + others)[0]


def body(control, diffusivity, perturb, vertical_filter, sub_widths, obs_raw, obs_counts, obs_rinv):
    members, levels_here, size_x, size_y = control.shape
    columns = size_x * size_y
    capacity = perturb.shape[1]
    levels = perturb.shape[2]
    groups = sub_widths.shape[0]
    obs_cap = obs_raw.shape[1]
    part = capacity // PARTS
    half = part // 2
    n_mem = lax.axis_size("mem")
    me = lax.axis_index("lev")
    smem = pl.BlockSpec(memory_space=pltpu.SMEM)
    params = pltpu.CompilerParams(vmem_limit_bytes=56 << 20)
    flat_width = columns + capacity + LANES
    piece_shape = jax.ShapeDtypeStruct((GROUP, part), F32)
    pieces_shape = jax.ShapeDtypeStruct((groups, levels_here, part), F32)
    group_shape = jax.ShapeDtypeStruct((groups, GROUP, part), F32)
    n_groups = levels_here // GROUP
    any_spec = pl.BlockSpec(memory_space=pl.ANY)

    def exchange(pieces):
        return lax.all_to_all(pieces, "lev", 0, 0, tiled=True)

    def permute(piece, turn):
        return lax.ppermute(piece, "lev", flip_pairs(groups, turn)) if turn else piece

    diffs, later, got = [], None, []
    for group in range(n_groups):
        before = [] if later is None else [later]
        n_sooner = groups if group else 1
        results = pl.pallas_call(
            functools.partial(forward_kernel, size_x, size_y, groups, n_sooner),
            grid=(1,),
            in_specs=[
                smem,
                pl.BlockSpec((1, GROUP, size_x, size_y), lambda g, group=group: (0, group, 0, 0)),
                pl.BlockSpec((GROUP, size_x, size_y), lambda g, group=group: (group, 0, 0)),
            ]
            + [any_spec] * len(before),
            out_specs=[
                pl.BlockSpec((size_x, GROUP, size_y), lambda g: (0, 0, 0)),
                pl.BlockSpec((groups, GROUP, part), lambda g, group=group: (0, group, 0)),
            ]
            + (
                [pl.BlockSpec((GROUP, part), lambda g: (0, 0))] * groups
                if group
                else [pl.BlockSpec((groups, GROUP, part), lambda g: (0, 0, 0))]
            ),
            out_shape=[jax.ShapeDtypeStruct((size_x, GROUP, size_y), F32), pieces_shape]
            + ([piece_shape] * groups if group else [group_shape]),
            input_output_aliases={3: 1} if before else {},
            scratch_shapes=[pltpu.VMEM((GROUP, flat_width), F32)]
            + [pltpu.VMEM((size_x, GROUP, size_y), F32)] * 5,
            compiler_params=params,
            cost_estimate=pl.CostEstimate(flops=0, bytes_accessed=0, transcendentals=0),
            name="smooth_and_cut",
        )(sub_widths, control, diffusivity, *before)
        diffs.append(results[0])
        later = results[1]
        if group:
            got += [permute(piece, turn) for piece, turn in zip(results[2:], turns_in(groups))]
        else:
            got.append(exchange(results[2]))

    width = sub_widths[me]
    live = jnp.arange(obs_cap, dtype=jnp.int32) < obs_counts[me]
    slots = jnp.where(live, obs_raw[0] % width, -1)[None, :]

    by_group = vertical_filter.reshape(levels, groups, n_groups, GROUP)
    def reordered(orders):
        places = [jnp.bitwise_xor(me, jnp.array(order, jnp.int32)) if order else jnp.arange(groups) for order in orders]
        return jnp.concatenate([by_group[:, at, g].reshape(levels, -1) for g, at in enumerate(places)], axis=1)

    last = n_groups - 1
    filter_in = reordered([turns_in(groups) if g else None for g in range(n_groups)])
    filter_out = reordered([turns_out(groups, g == last) for g in range(n_groups)])

    width = half
    blocks = part // width
    some = blocks // 2

    def block_of(g, core):
        return (g // some + core[0]) % 2 * some + g % some

    square = pl.BlockSpec((levels, levels), lambda g, core: (0, 0))
    slab = pl.BlockSpec((groups, levels_here, width), lambda g, core: (0, 0, block_of(g, core)))
    strip = pl.BlockSpec((GROUP, width), lambda g, core: (0, block_of(g, core)))
    group_slab = pl.BlockSpec((groups, GROUP, width), lambda g, core: (0, 0, block_of(g, core)))
    strips_in = [group_slab] + [strip] * (groups * (n_groups - 1))
    first_half = pl.BlockSpec((width, levels), lambda g, core: (jnp.minimum(g, some - 1), 0))
    second_half = pl.BlockSpec((width, levels), lambda g, core: (jnp.maximum(g - some, 0), 0))
    half_shape = jax.ShapeDtypeStruct((half, levels), F32)
    core = (lax.axis_index("mem") % 2).astype(jnp.int32)[None]
    table = pltpu.VMEM((2 * levels, 2 * levels), BF16)
    cost = pl.CostEstimate(flops=0, bytes_accessed=0, transcendentals=0)
    rows_here = 256

    def weights(c, slots):
        return pl.pallas_call(
            functools.partial(observation_kernel, part, c, obs_cap),
            grid=(half // rows_here,),
            in_specs=[
                pl.BlockSpec((1, obs_cap), lambda g: (0, 0)),
                pl.BlockSpec((1, obs_cap, levels), lambda g: (0, 0, 0)),
            ],
            out_specs=pl.BlockSpec((rows_here, levels), lambda g: (g, 0)),
            out_shape=jax.ShapeDtypeStruct((half, levels), F32),
            scratch_shapes=[pltpu.VMEM((obs_cap, 2 * levels), BF16)],
            compiler_params=params,
            cost_estimate=cost,
            name="observation_weights",
        )(slots, obs_rinv)

    def perturb_part(c):
        return pl.BlockSpec((1, width, levels), lambda g, core: (0, c * blocks + block_of(g, core), 0))

    def filter_forward(c, vfilter, *pieces):
        return pl.pallas_call(
            filter_kernel,
            grid_spec=pltpu.PrefetchScalarGridSpec(
                num_scalar_prefetch=1,
                grid=(blocks,),
                in_specs=[square, perturb_part(c)] + ([slab] if len(pieces) == 1 else strips_in),
                out_specs=[first_half, second_half],
                scratch_shapes=[table],
            ),
            out_shape=[half_shape, half_shape],
            compiler_params=params,
            cost_estimate=cost,
            name="filter_forward",
        )(core, vfilter, perturb, *pieces)

    def filter_backward(c, vfilter, adj_mine, adj_other, strips):
        return pl.pallas_call(
            functools.partial(back_kernel, len(adj_mine)),
            grid_spec=pltpu.PrefetchScalarGridSpec(
                num_scalar_prefetch=1,
                grid=(blocks,),
                in_specs=[square, perturb_part(c)]
                + [pl.BlockSpec(adj.shape, lambda g, core: (0, 0)) for adj in adj_mine + adj_other],
                out_specs=[strip] * (groups * n_groups) if strips else [slab],
                scratch_shapes=[table],
            ),
            out_shape=[piece_shape] * (groups * n_groups) if strips else [pieces_shape],
            compiler_params=params,
            cost_estimate=cost,
            name="filter_backward",
        )(core, vfilter, perturb, *adj_mine, *adj_other)

    def member_sum(keep, send, obs_weight, pieces):
        mine, other = [], []
        for first in range(0, half, half // pieces):
            here = slice(first, first + half // pieces)
            total = keep[here] + lax.ppermute(send[here], "mem", flip_pairs(n_mem, 1))
            bit = 2
            while bit < n_mem:
                total = total + lax.ppermute(total, "mem", flip_pairs(n_mem, bit))
                bit *= 2
            mine.append(total * obs_weight[here])
            other.append(lax.ppermute(mine[-1], "mem", flip_pairs(n_mem, 1)))
        return mine, other

    slots = after(slots, got[1], filter_out)
    weight = [weights(c, slots) for c in range(PARTS)]
    got_later = exchange(later)

    keep, send = filter_forward(0, filter_in, *got)
    mine, other = member_sum(keep, send, weight[0], 1)
    pieces = filter_backward(0, vertical_filter, mine, other, False)[0]
    back_sooner = exchange(pieces)

    keep, send = filter_forward(1, after(vertical_filter, pieces), got_later)
    mine, other = member_sum(keep, send, weight[1], 2)
    pieces = filter_backward(1, filter_out, mine, other, True)
    out = None
    for group in range(n_groups):
        before = [] if out is None else [out]
        back = []
        for piece, turn in zip(pieces[group * groups :], turns_out(groups, group == last)):
            back.append(permute(after(piece, out) if before and turn == 2 else piece, turn))
        out = pl.pallas_call(
            functools.partial(backward_kernel, size_x, size_y, groups, capacity, group, group == last),
            grid=(1,),
            in_specs=[smem, pl.BlockSpec((size_x, GROUP, size_y), lambda g: (0, 0, 0))]
            + [any_spec] * (1 + len(back) + len(before)),
            out_specs=pl.BlockSpec((1, GROUP, size_x, size_y), lambda g, group=group: (0, group, 0, 0)),
            out_shape=jax.ShapeDtypeStruct((members, levels_here, size_x, size_y), F32),
            input_output_aliases={3 + len(back): 0} if before else {},
            scratch_shapes=[
                pltpu.VMEM((groups, GROUP, capacity), F32),
                pltpu.VMEM((GROUP, flat_width), F32),
            ]
            + [pltpu.VMEM((size_x, GROUP, size_y), F32)] * 5
            + [pltpu.SemaphoreType.DMA((1 + groups,))],
            compiler_params=params,
            cost_estimate=pl.CostEstimate(flops=0, bytes_accessed=0, transcendentals=0),
            name="place_and_smooth",
        )(sub_widths, diffs[group], back_sooner, *back, *before)
    return out


def solution(mesh):
    return jax.shard_map(
        body,
        mesh=mesh,
        in_specs=(
            P("mem", "lev", None, None),
            P("lev", None, None),
            P("mem", "lev", None),
            P(),
            P(),
            P("lev", None),
            P(),
            P("lev", None, None),
        ),
        out_specs=P("mem", "lev", None, None),
        check_vma=False,
    )
```

```python
import functools

import jax
import jax.numpy as jnp
from jax import lax
from jax.experimental import pallas as pl
from jax.experimental.pallas import tpu as pltpu
from jax.sharding import PartitionSpec as P

STEPS = 4
PARTS = 2
LANES = 128
GROUP = 8
F32 = jnp.float32
BF16 = jnp.bfloat16


def flip_pairs(size, bit):
    return [(i, i ^ bit) for i in range(size)]


def transpose_in(src, dst, size_x):
    def step(b, _):
        first = pl.multiple_of(b * 8, 8)
        dst[pl.ds(first, 8)] = jnp.swapaxes(src[:, pl.ds(first, 8), :], 0, 1)
        return 0

    lax.fori_loop(0, size_x // 8, step, 0, unroll=2)


def faces(diff, face_x, face_up, face_down, size_x, size_y):
    lane = lax.broadcasted_iota(jnp.int32, (1, GROUP, size_y), 2)
    rows = 8

    def step(b, _):
        first = pl.multiple_of(b * rows, rows)
        here = diff[pl.ds(first, rows)]
        beyond = diff[pl.ds(jnp.minimum(first + rows, size_x - 1), 1)]
        ahead = jnp.concatenate([here[1:], beyond], axis=0)
        face_x[pl.ds(first, rows)] = 0.5 * (here + ahead)
        up = 0.5 * (here + pltpu.roll(here, size_y - 1, 2))
        face_up[pl.ds(first, rows)] = jnp.where(lane < size_y - 1, up, 0.0)
        down = 0.5 * (here + pltpu.roll(here, 1, 2))
        face_down[pl.ds(first, rows)] = jnp.where(lane > 0, down, 0.0)
        return 0

    lax.fori_loop(0, size_x // rows, step, 0, unroll=16)
    face_x[size_x - 1] = jnp.zeros((GROUP, size_y), F32)


def sweep(read, write, face_x, face_up, face_down, size_x, size_y):
    rows = 8

    def step(b, flux_before):
        first = pl.multiple_of(b * rows, rows)
        here = read(first, rows)
        beyond = read(jnp.minimum(first + rows, size_x - 1), 1)
        ahead = jnp.concatenate([here[1:], beyond], axis=0)
        flux_x = face_x[pl.ds(first, rows)] * (ahead - here)
        flux_up = face_up[pl.ds(first, rows)] * (pltpu.roll(here, size_y - 1, 2) - here)
        flux_down = face_down[pl.ds(first, rows)] * (here - pltpu.roll(here, 1, 2))
        behind = jnp.concatenate([flux_before, flux_x[:-1]], axis=0)
        write(first, rows, here + (flux_x - behind) + (flux_up - flux_down))
        return flux_x[-1:]

    lax.fori_loop(0, size_x // rows, step, jnp.zeros((1, GROUP, size_y), F32), unroll=16)


def on_grid(grid):
    def read(first, rows):
        return grid[pl.ds(first, rows)]

    def write(first, rows, value):
        grid[pl.ds(first, rows)] = value

    return read, write


def on_flat(flat, size_y):
    def at(x):
        return pl.ds(pl.multiple_of(x * size_y, size_y), size_y)

    def read(first, rows):
        return jnp.stack([flat[:, at(first + i)] for i in range(rows)], axis=0)

    def write(first, rows, value):
        for i in range(rows):
            flat[:, at(first + i)] = value[i]

    return read, write


def start_of(widths, j):
    return lax.fori_loop(0, j, lambda k, total: total + widths[k], jnp.int32(0))


def turns_in(groups):
    return list(range(groups))


def turns_out(groups, last):
    near, far = list(range(groups // 2 - 1, 1, -1)), list(range(groups // 2, groups))
    return [0] + near[:1] + far + near[1:] + [1] if last else [0] + far + near + [1]


def forward_kernel(size_x, size_y, groups, n_sooner, widths, control, diffusivity, *rest):
    *rest, flat, one, two, face_x, face_up, face_down = rest
    diff_out, later, *sooner = rest[-n_sooner - 2 :]
    face_refs = (face_x, face_up, face_down)
    columns = size_x * size_y
    part = later.shape[2]
    transpose_in(diffusivity, diff_out, size_x)
    faces(diff_out, *face_refs, size_x, size_y)
    transpose_in(control.at[0], one, size_x)
    stages = [on_grid((one, two)[i % 2]) for i in range(STEPS)] + [on_flat(flat, size_y)]
    for i in range(STEPS):
        sweep(stages[i][0], stages[i + 1][1], *face_refs, size_x, size_y)
    flat[:, columns:] = jnp.zeros((GROUP, flat.shape[1] - columns), F32)

    lane = lax.broadcasted_iota(jnp.int32, (GROUP, LANES), 1)
    me = lax.axis_index("lev")
    tiles = part // LANES

    def cut(j, c, store):
        start = start_of(widths, j)
        base = start // LANES
        shift = start - base * LANES
        back = lax.rem(LANES - shift, LANES)
        low = lane < LANES - shift
        begin = base + c * tiles

        def load(t):
            at = pl.multiple_of((begin + t) * LANES, LANES)
            return pltpu.roll(flat[:, pl.ds(at, LANES)], back, 1)

        now = load(0)
        for t in range(tiles):
            following = load(t + 1)
            store(t, jnp.where(low, now, following))
            now = following

    for d, turn in enumerate(turns_in(groups)):

        def store_sooner(t, value):
            target = sooner[d] if n_sooner == groups else sooner[0].at[d]
            target[:, t * LANES : (t + 1) * LANES] = value

        def store_later(t, value):
            later[d, :, t * LANES : (t + 1) * LANES] = value

        cut(jnp.bitwise_xor(me, turn) if n_sooner == groups else d, 0, store_sooner)
        cut(d, 1, store_later)


def split2(value):
    high = value.astype(BF16)
    return high, (value - high.astype(F32)).astype(BF16)


def observation_kernel(part_rows, index, obs_cap, slots, rinv, out, split):
    step = pl.program_id(0)
    rows_here, levels = out.shape

    @pl.when(step == 0)
    def _():
        high, low = split2(rinv[0])
        split[:, :levels] = high
        split[:, levels:] = low

    core = lax.axis_index("mem") % 2
    first = index * part_rows + core * (part_rows // 2) + step * rows_here
    row = first + lax.broadcasted_iota(jnp.int32, (rows_here, obs_cap), 0)
    onehot = jnp.where(row == slots[...], 1.0, 0.0).astype(BF16)
    total = jnp.dot(onehot, split[...], preferred_element_type=F32)
    out[...] = total[:, :levels] + total[:, levels:]


def filter_kernel(core, vfilter, perturb, *rest):
    *pieces, keep, send, table = rest
    levels = vfilter.shape[0]
    rows = keep.shape[0]
    step = pl.program_id(0)
    blocks = pl.num_programs(0) // 2

    @pl.when(step == 0)
    def _():
        high, low = split2(vfilter[...].T)
        table[:levels, :levels] = high
        table[levels:, :levels] = high
        table[:levels, levels:] = low
        table[levels:, levels:] = jnp.zeros_like(low)

    slab = jnp.concatenate([piece[...].reshape(-1, rows) for piece in pieces], axis=0)
    both = jnp.concatenate(split2(slab.T), axis=1)
    products = jnp.dot(both, table[...], preferred_element_type=F32)
    result = perturb[0] * (products[:, :levels] + products[:, levels:])

    @pl.when(step < blocks)
    def _():
        keep[...] = result

    @pl.when(step >= blocks)
    def _():
        send[...] = result


def back_kernel(n_adj, core, vfilter, perturb, *rest):
    adj_mine, adj_other = rest[:n_adj], rest[n_adj : 2 * n_adj]
    *pieces, table = rest[2 * n_adj :]
    levels = vfilter.shape[0]
    step = pl.program_id(0)
    blocks = pl.num_programs(0) // 2

    @pl.when(step == 0)
    def _():
        high, low = split2(vfilter[...])
        table[:levels, :levels] = high
        table[levels:, :levels] = high
        table[:levels, levels:] = low
        table[levels:, levels:] = jnp.zeros_like(low)

    adj = jnp.concatenate([jnp.where(step < blocks, a[...], b[...]) for a, b in zip(adj_mine, adj_other)], axis=0)
    both = jnp.concatenate(split2(perturb[0] * adj), axis=1)
    products = jnp.dot(both, table[...], preferred_element_type=F32)
    result = (products[:, :levels] + products[:, levels:]).T
    first = 0
    for piece in pieces:
        count = piece.size // piece.shape[-1]
        piece[...] = result[first : first + count].reshape(piece.shape)
        first += count


def backward_kernel(size_x, size_y, groups, capacity, group, last, widths, diff, *rest):
    *rest, staging, flat, one, two, face_x, face_up, face_down, sem = rest
    face_refs = (face_x, face_up, face_down)
    sooner, *later = rest[: groups + 1]
    out = rest[-1]
    part = capacity // PARTS
    me = lax.axis_index("lev")
    copies = [
        pltpu.make_async_copy(
            sooner.at[:, pl.ds(group * GROUP, GROUP), :], staging.at[:, :, pl.ds(0, part)], sem.at[0]
        )
    ]
    late = pl.ds(part, part)
    targets = [staging.at[jnp.bitwise_xor(me, turn), :, late] for turn in turns_out(groups, last)]
    for d in range(groups):
        copies.append(pltpu.make_async_copy(later[d], targets[d], sem.at[1 + d]))
    for copy in copies:
        copy.start()
    faces(diff, *face_refs, size_x, size_y)
    for copy in copies:
        copy.wait()

    lane = lax.broadcasted_iota(jnp.int32, (GROUP, LANES), 1)
    tiles = capacity // LANES

    def place(j, _):
        start = start_of(widths, j)
        base = start // LANES
        shift = start - base * LANES
        high = lane >= shift

        before = flat[:, pl.ds(pl.multiple_of(base * LANES, LANES), LANES)]
        for t in range(tiles):
            to = pl.multiple_of((base + t) * LANES, LANES)
            here = pltpu.roll(staging[j, :, t * LANES : (t + 1) * LANES], shift, 1)
            flat[:, pl.ds(to, LANES)] = jnp.where(high, here, before)
            before = here
        flat[:, pl.ds(pl.multiple_of((base + tiles) * LANES, LANES), LANES)] = before
        return 0

    lax.fori_loop(0, groups, place, 0)

    stages = [on_flat(flat, size_y)] + [on_grid((one, two)[i % 2]) for i in range(STEPS)]
    for i in range(STEPS):
        sweep(stages[i][0], stages[i + 1][1], *face_refs, size_x, size_y)
    grid = (one, two)[(STEPS - 1) % 2]

    def back(b, _):
        first = pl.multiple_of(b * 8, 8)
        out[0, :, pl.ds(first, 8), :] = jnp.swapaxes(grid[pl.ds(first, 8)], 0, 1)
        return 0

    lax.fori_loop(0, size_x // 8, back, 0, unroll=2)


def after(value, *others):
    return lax.optimization_barrier((value,) + others)[0]


def body(control, diffusivity, perturb, vertical_filter, sub_widths, obs_raw, obs_counts, obs_rinv):
    members, levels_here, size_x, size_y = control.shape
    columns = size_x * size_y
    capacity = perturb.shape[1]
    levels = perturb.shape[2]
    groups = sub_widths.shape[0]
    obs_cap = obs_raw.shape[1]
    part = capacity // PARTS
    half = part // 2
    n_mem = lax.axis_size("mem")
    me = lax.axis_index("lev")
    smem = pl.BlockSpec(memory_space=pltpu.SMEM)
    params = pltpu.CompilerParams(vmem_limit_bytes=56 << 20)
    flat_width = columns + capacity + LANES
    piece_shape = jax.ShapeDtypeStruct((GROUP, part), F32)
    pieces_shape = jax.ShapeDtypeStruct((groups, levels_here, part), F32)
    group_shape = jax.ShapeDtypeStruct((groups, GROUP, part), F32)
    n_groups = levels_here // GROUP
    any_spec = pl.BlockSpec(memory_space=pl.ANY)

    def exchange(pieces):
        return lax.all_to_all(pieces, "lev", 0, 0, tiled=True)

    def permute(piece, turn):
        return lax.ppermute(piece, "lev", flip_pairs(groups, turn)) if turn else piece

    diffs, later, got = [], None, []
    for group in range(n_groups):
        before = [] if later is None else [later]
        n_sooner = groups if group else 1
        results = pl.pallas_call(
            functools.partial(forward_kernel, size_x, size_y, groups, n_sooner),
            grid=(1,),
            in_specs=[
                smem,
                pl.BlockSpec((1, GROUP, size_x, size_y), lambda g, group=group: (0, group, 0, 0)),
                pl.BlockSpec((GROUP, size_x, size_y), lambda g, group=group: (group, 0, 0)),
            ]
            + [any_spec] * len(before),
            out_specs=[
                pl.BlockSpec((size_x, GROUP, size_y), lambda g: (0, 0, 0)),
                pl.BlockSpec((groups, GROUP, part), lambda g, group=group: (0, group, 0)),
            ]
            + (
                [pl.BlockSpec((GROUP, part), lambda g: (0, 0))] * groups
                if group
                else [pl.BlockSpec((groups, GROUP, part), lambda g: (0, 0, 0))]
            ),
            out_shape=[jax.ShapeDtypeStruct((size_x, GROUP, size_y), F32), pieces_shape]
            + ([piece_shape] * groups if group else [group_shape]),
            input_output_aliases={3: 1} if before else {},
            scratch_shapes=[pltpu.VMEM((GROUP, flat_width), F32)]
            + [pltpu.VMEM((size_x, GROUP, size_y), F32)] * 5,
            compiler_params=params,
            cost_estimate=pl.CostEstimate(flops=0, bytes_accessed=0, transcendentals=0),
            name="smooth_and_cut",
        )(sub_widths, control, diffusivity, *before)
        diffs.append(results[0])
        later = results[1]
        if group:
            got += [permute(piece, turn) for piece, turn in zip(results[2:], turns_in(groups))]
        else:
            got.append(exchange(results[2]))

    width = sub_widths[me]
    live = jnp.arange(obs_cap, dtype=jnp.int32) < obs_counts[me]
    slots = jnp.where(live, obs_raw[0] % width, -1)[None, :]

    by_group = vertical_filter.reshape(levels, groups, n_groups, GROUP)
    def reordered(orders):
        places = [jnp.bitwise_xor(me, jnp.array(order, jnp.int32)) if order else jnp.arange(groups) for order in orders]
        return jnp.concatenate([by_group[:, at, g].reshape(levels, -1) for g, at in enumerate(places)], axis=1)

    last = n_groups - 1
    filter_in = reordered([turns_in(groups) if g else None for g in range(n_groups)])
    filter_out = reordered([turns_out(groups, g == last) for g in range(n_groups)])

    width = half
    blocks = part // width
    some = blocks // 2

    def block_of(g, core):
        return (g // some + core[0]) % 2 * some + g % some

    square = pl.BlockSpec((levels, levels), lambda g, core: (0, 0))
    slab = pl.BlockSpec((groups, levels_here, width), lambda g, core: (0, 0, block_of(g, core)))
    strip = pl.BlockSpec((GROUP, width), lambda g, core: (0, block_of(g, core)))
    group_slab = pl.BlockSpec((groups, GROUP, width), lambda g, core: (0, 0, block_of(g, core)))
    strips_in = [group_slab] + [strip] * (groups * (n_groups - 1))
    first_half = pl.BlockSpec((width, levels), lambda g, core: (jnp.minimum(g, some - 1), 0))
    second_half = pl.BlockSpec((width, levels), lambda g, core: (jnp.maximum(g - some, 0), 0))
    half_shape = jax.ShapeDtypeStruct((half, levels), F32)
    core = (lax.axis_index("mem") % 2).astype(jnp.int32)[None]
    table = pltpu.VMEM((2 * levels, 2 * levels), BF16)
    cost = pl.CostEstimate(flops=0, bytes_accessed=0, transcendentals=0)
    rows_here = 256

    def weights(c, slots):
        return pl.pallas_call(
            functools.partial(observation_kernel, part, c, obs_cap),
            grid=(half // rows_here,),
            in_specs=[
                pl.BlockSpec((1, obs_cap), lambda g: (0, 0)),
                pl.BlockSpec((1, obs_cap, levels), lambda g: (0, 0, 0)),
            ],
            out_specs=pl.BlockSpec((rows_here, levels), lambda g: (g, 0)),
            out_shape=jax.ShapeDtypeStruct((half, levels), F32),
            scratch_shapes=[pltpu.VMEM((obs_cap, 2 * levels), BF16)],
            compiler_params=params,
            cost_estimate=cost,
            name="observation_weights",
        )(slots, obs_rinv)

    def perturb_part(c):
        return pl.BlockSpec((1, width, levels), lambda g, core: (0, c * blocks + block_of(g, core), 0))

    def filter_forward(c, vfilter, *pieces):
        return pl.pallas_call(
            filter_kernel,
            grid_spec=pltpu.PrefetchScalarGridSpec(
                num_scalar_prefetch=1,
                grid=(blocks,),
                in_specs=[square, perturb_part(c)] + ([slab] if len(pieces) == 1 else strips_in),
                out_specs=[first_half, second_half],
                scratch_shapes=[table],
            ),
            out_shape=[half_shape, half_shape],
            compiler_params=params,
            cost_estimate=cost,
            name="filter_forward",
        )(core, vfilter, perturb, *pieces)

    def filter_backward(c, vfilter, adj_mine, adj_other, strips):
        return pl.pallas_call(
            functools.partial(back_kernel, len(adj_mine)),
            grid_spec=pltpu.PrefetchScalarGridSpec(
                num_scalar_prefetch=1,
                grid=(blocks,),
                in_specs=[square, perturb_part(c)]
                + [pl.BlockSpec(adj.shape, lambda g, core: (0, 0)) for adj in adj_mine + adj_other],
                out_specs=[strip] * (groups * n_groups) if strips else [slab],
                scratch_shapes=[table],
            ),
            out_shape=[piece_shape] * (groups * n_groups) if strips else [pieces_shape],
            compiler_params=params,
            cost_estimate=cost,
            name="filter_backward",
        )(core, vfilter, perturb, *adj_mine, *adj_other)

    def member_sum(keep, send, obs_weight, pieces):
        mine, other = [], []
        for first in range(0, half, half // pieces):
            here = slice(first, first + half // pieces)
            total = keep[here] + lax.ppermute(send[here], "mem", flip_pairs(n_mem, 1))
            bit = 2
            while bit < n_mem:
                total = total + lax.ppermute(total, "mem", flip_pairs(n_mem, bit))
                bit *= 2
            mine.append(total * obs_weight[here])
            other.append(lax.ppermute(mine[-1], "mem", flip_pairs(n_mem, 1)))
        return mine, other

    slots = after(slots, got[1], filter_out)
    weight = [weights(c, slots) for c in range(PARTS)]
    got_later = exchange(later)

    keep, send = filter_forward(0, filter_in, *got)
    mine, other = member_sum(keep, send, weight[0], 1)
    pieces = filter_backward(0, vertical_filter, mine, other, False)[0]
    back_sooner = exchange(pieces)

    keep, send = filter_forward(1, after(vertical_filter, pieces), got_later)
    mine, other = member_sum(keep, send, weight[1], 2)
    pieces = filter_backward(1, filter_out, mine, other, True)
    out = None
    for group in range(n_groups):
        before = [] if out is None else [out]
        back = []
        for piece, turn in zip(pieces[group * groups :], turns_out(groups, group == last)):
            back.append(permute(after(piece, out) if before and turn == 1 else piece, turn))
        out = pl.pallas_call(
            functools.partial(backward_kernel, size_x, size_y, groups, capacity, group, group == last),
            grid=(1,),
            in_specs=[smem, pl.BlockSpec((size_x, GROUP, size_y), lambda g: (0, 0, 0))]
            + [any_spec] * (1 + len(back) + len(before)),
            out_specs=pl.BlockSpec((1, GROUP, size_x, size_y), lambda g, group=group: (0, group, 0, 0)),
            out_shape=jax.ShapeDtypeStruct((members, levels_here, size_x, size_y), F32),
            input_output_aliases={3 + len(back): 0} if before else {},
            scratch_shapes=[
                pltpu.VMEM((groups, GROUP, capacity), F32),
                pltpu.VMEM((GROUP, flat_width), F32),
            ]
            + [pltpu.VMEM((size_x, GROUP, size_y), F32)] * 5
            + [pltpu.SemaphoreType.DMA((1 + groups,))],
            compiler_params=params,
            cost_estimate=pl.CostEstimate(flops=0, bytes_accessed=0, transcendentals=0),
            name="place_and_smooth",
        )(sub_widths, diffs[group], back_sooner, *back, *before)
    return out


def solution(mesh):
    return jax.shard_map(
        body,
        mesh=mesh,
        in_specs=(
            P("mem", "lev", None, None),
            P("lev", None, None),
            P("mem", "lev", None),
            P(),
            P(),
            P("lev", None),
            P(),
            P("lev", None, None),
        ),
        out_specs=P("mem", "lev", None, None),
        check_vma=False,
    )
```

```python
import functools

import jax
import jax.numpy as jnp
from jax import lax
from jax.experimental import pallas as pl
from jax.experimental.pallas import tpu as pltpu
from jax.sharding import PartitionSpec as P

STEPS = 4
PARTS = 2
LANES = 128
GROUP = 8
F32 = jnp.float32
BF16 = jnp.bfloat16


def flip_pairs(size, bit):
    return [(i, i ^ bit) for i in range(size)]


def transpose_in(src, dst, size_x):
    def step(b, _):
        first = pl.multiple_of(b * 8, 8)
        dst[pl.ds(first, 8)] = jnp.swapaxes(src[:, pl.ds(first, 8), :], 0, 1)
        return 0

    lax.fori_loop(0, size_x // 8, step, 0, unroll=8)


def faces(diff, face_x, face_up, face_down, size_x, size_y):
    lane = lax.broadcasted_iota(jnp.int32, (1, GROUP, size_y), 2)
    rows = 8

    def step(b, _):
        first = pl.multiple_of(b * rows, rows)
        here = diff[pl.ds(first, rows)]
        beyond = diff[pl.ds(jnp.minimum(first + rows, size_x - 1), 1)]
        ahead = jnp.concatenate([here[1:], beyond], axis=0)
        face_x[pl.ds(first, rows)] = 0.5 * (here + ahead)
        up = 0.5 * (here + pltpu.roll(here, size_y - 1, 2))
        face_up[pl.ds(first, rows)] = jnp.where(lane < size_y - 1, up, 0.0)
        down = 0.5 * (here + pltpu.roll(here, 1, 2))
        face_down[pl.ds(first, rows)] = jnp.where(lane > 0, down, 0.0)
        return 0

    lax.fori_loop(0, size_x // rows, step, 0, unroll=16)
    face_x[size_x - 1] = jnp.zeros((GROUP, size_y), F32)


def sweep(read, write, face_x, face_up, face_down, size_x, size_y):
    rows = 8

    def step(b, flux_before):
        first = pl.multiple_of(b * rows, rows)
        here = read(first, rows)
        beyond = read(jnp.minimum(first + rows, size_x - 1), 1)
        ahead = jnp.concatenate([here[1:], beyond], axis=0)
        flux_x = face_x[pl.ds(first, rows)] * (ahead - here)
        flux_up = face_up[pl.ds(first, rows)] * (pltpu.roll(here, size_y - 1, 2) - here)
        flux_down = face_down[pl.ds(first, rows)] * (here - pltpu.roll(here, 1, 2))
        behind = jnp.concatenate([flux_before, flux_x[:-1]], axis=0)
        write(first, rows, here + (flux_x - behind) + (flux_up - flux_down))
        return flux_x[-1:]

    lax.fori_loop(0, size_x // rows, step, jnp.zeros((1, GROUP, size_y), F32), unroll=16)


def on_grid(grid):
    def read(first, rows):
        return grid[pl.ds(first, rows)]

    def write(first, rows, value):
        grid[pl.ds(first, rows)] = value

    return read, write


def on_flat(flat, size_y):
    def at(x):
        return pl.ds(pl.multiple_of(x * size_y, size_y), size_y)

    def read(first, rows):
        return jnp.stack([flat[:, at(first + i)] for i in range(rows)], axis=0)

    def write(first, rows, value):
        for i in range(rows):
            flat[:, at(first + i)] = value[i]

    return read, write


def start_of(widths, j):
    return lax.fori_loop(0, j, lambda k, total: total + widths[k], jnp.int32(0))


def turns_in(groups):
    return list(range(groups))


def turns_out(groups, last):
    near, far = list(range(groups // 2 - 1, 1, -1)), list(range(groups // 2, groups))
    return [0] + near[:1] + far + near[1:] + [1] if last else [0] + far + near + [1]


def forward_kernel(size_x, size_y, groups, n_sooner, widths, control, diffusivity, *rest):
    *rest, flat, one, two, face_x, face_up, face_down = rest
    diff_out, later, *sooner = rest[-n_sooner - 2 :]
    face_refs = (face_x, face_up, face_down)
    columns = size_x * size_y
    part = later.shape[2]
    transpose_in(diffusivity, diff_out, size_x)
    faces(diff_out, *face_refs, size_x, size_y)
    transpose_in(control.at[0], one, size_x)
    stages = [on_grid((one, two)[i % 2]) for i in range(STEPS)] + [on_flat(flat, size_y)]
    for i in range(STEPS):
        sweep(stages[i][0], stages[i + 1][1], *face_refs, size_x, size_y)
    flat[:, columns:] = jnp.zeros((GROUP, flat.shape[1] - columns), F32)

    lane = lax.broadcasted_iota(jnp.int32, (GROUP, LANES), 1)
    me = lax.axis_index("lev")
    tiles = part // LANES

    def cut(j, c, store):
        start = start_of(widths, j)
        base = start // LANES
        shift = start - base * LANES
        back = lax.rem(LANES - shift, LANES)
        low = lane < LANES - shift
        begin = base + c * tiles

        def load(t):
            at = pl.multiple_of((begin + t) * LANES, LANES)
            return pltpu.roll(flat[:, pl.ds(at, LANES)], back, 1)

        now = load(0)
        for t in range(tiles):
            following = load(t + 1)
            store(t, jnp.where(low, now, following))
            now = following

    for d, turn in enumerate(turns_in(groups)):

        def store_sooner(t, value):
            target = sooner[d] if n_sooner == groups else sooner[0].at[d]
            target[:, t * LANES : (t + 1) * LANES] = value

        def store_later(t, value):
            later[d, :, t * LANES : (t + 1) * LANES] = value

        cut(jnp.bitwise_xor(me, turn) if n_sooner == groups else d, 0, store_sooner)
        cut(d, 1, store_later)


def split2(value):
    high = value.astype(BF16)
    return high, (value - high.astype(F32)).astype(BF16)


def observation_kernel(part_rows, index, obs_cap, slots, rinv, out, split):
    step = pl.program_id(0)
    rows_here, levels = out.shape

    @pl.when(step == 0)
    def _():
        high, low = split2(rinv[0])
        split[:, :levels] = high
        split[:, levels:] = low

    core = lax.axis_index("mem") % 2
    first = index * part_rows + core * (part_rows // 2) + step * rows_here
    row = first + lax.broadcasted_iota(jnp.int32, (rows_here, obs_cap), 0)
    onehot = jnp.where(row == slots[...], 1.0, 0.0).astype(BF16)
    total = jnp.dot(onehot, split[...], preferred_element_type=F32)
    out[...] = total[:, :levels] + total[:, levels:]


def filter_kernel(core, vfilter, perturb, *rest):
    *pieces, keep, send, table = rest
    levels = vfilter.shape[0]
    rows = keep.shape[0]
    step = pl.program_id(0)
    blocks = pl.num_programs(0) // 2

    @pl.when(step == 0)
    def _():
        high, low = split2(vfilter[...].T)
        table[:levels, :levels] = high
        table[levels:, :levels] = high
        table[:levels, levels:] = low
        table[levels:, levels:] = jnp.zeros_like(low)

    slab = jnp.concatenate([piece[...].reshape(-1, rows) for piece in pieces], axis=0)
    both = jnp.concatenate(split2(slab.T), axis=1)
    products = jnp.dot(both, table[...], preferred_element_type=F32)
    result = perturb[0] * (products[:, :levels] + products[:, levels:])

    @pl.when(step < blocks)
    def _():
        keep[...] = result

    @pl.when(step >= blocks)
    def _():
        send[...] = result


def back_kernel(n_adj, core, vfilter, perturb, *rest):
    adj_mine, adj_other = rest[:n_adj], rest[n_adj : 2 * n_adj]
    *pieces, table = rest[2 * n_adj :]
    levels = vfilter.shape[0]
    step = pl.program_id(0)
    blocks = pl.num_programs(0) // 2

    @pl.when(step == 0)
    def _():
        high, low = split2(vfilter[...])
        table[:levels, :levels] = high
        table[levels:, :levels] = high
        table[:levels, levels:] = low
        table[levels:, levels:] = jnp.zeros_like(low)

    adj = jnp.concatenate([jnp.where(step < blocks, a[...], b[...]) for a, b in zip(adj_mine, adj_other)], axis=0)
    both = jnp.concatenate(split2(perturb[0] * adj), axis=1)
    products = jnp.dot(both, table[...], preferred_element_type=F32)
    result = (products[:, :levels] + products[:, levels:]).T
    first = 0
    for piece in pieces:
        count = piece.size // piece.shape[-1]
        piece[...] = result[first : first + count].reshape(piece.shape)
        first += count


def backward_kernel(size_x, size_y, groups, capacity, group, last, widths, diff, *rest):
    *rest, staging, flat, one, two, face_x, face_up, face_down, sem = rest
    face_refs = (face_x, face_up, face_down)
    sooner, *later = rest[: groups + 1]
    out = rest[-1]
    part = capacity // PARTS
    me = lax.axis_index("lev")
    copies = [
        pltpu.make_async_copy(
            sooner.at[:, pl.ds(group * GROUP, GROUP), :], staging.at[:, :, pl.ds(0, part)], sem.at[0]
        )
    ]
    late = pl.ds(part, part)
    targets = [staging.at[jnp.bitwise_xor(me, turn), :, late] for turn in turns_out(groups, last)]
    for d in range(groups):
        copies.append(pltpu.make_async_copy(later[d], targets[d], sem.at[1 + d]))
    for copy in copies:
        copy.start()
    faces(diff, *face_refs, size_x, size_y)
    for copy in copies:
        copy.wait()

    lane = lax.broadcasted_iota(jnp.int32, (GROUP, LANES), 1)
    tiles = capacity // LANES

    def place(j, _):
        start = start_of(widths, j)
        base = start // LANES
        shift = start - base * LANES
        high = lane >= shift

        before = flat[:, pl.ds(pl.multiple_of(base * LANES, LANES), LANES)]
        for t in range(tiles):
            to = pl.multiple_of((base + t) * LANES, LANES)
            here = pltpu.roll(staging[j, :, t * LANES : (t + 1) * LANES], shift, 1)
            flat[:, pl.ds(to, LANES)] = jnp.where(high, here, before)
            before = here
        flat[:, pl.ds(pl.multiple_of((base + tiles) * LANES, LANES), LANES)] = before
        return 0

    lax.fori_loop(0, groups, place, 0)

    stages = [on_flat(flat, size_y)] + [on_grid((one, two)[i % 2]) for i in range(STEPS)]
    for i in range(STEPS):
        sweep(stages[i][0], stages[i + 1][1], *face_refs, size_x, size_y)
    grid = (one, two)[(STEPS - 1) % 2]

    def back(b, _):
        first = pl.multiple_of(b * 8, 8)
        out[0, :, pl.ds(first, 8), :] = jnp.swapaxes(grid[pl.ds(first, 8)], 0, 1)
        return 0

    lax.fori_loop(0, size_x // 8, back, 0, unroll=2)


def after(value, *others):
    return lax.optimization_barrier((value,) + others)[0]


def body(control, diffusivity, perturb, vertical_filter, sub_widths, obs_raw, obs_counts, obs_rinv):
    members, levels_here, size_x, size_y = control.shape
    columns = size_x * size_y
    capacity = perturb.shape[1]
    levels = perturb.shape[2]
    groups = sub_widths.shape[0]
    obs_cap = obs_raw.shape[1]
    part = capacity // PARTS
    half = part // 2
    n_mem = lax.axis_size("mem")
    me = lax.axis_index("lev")
    smem = pl.BlockSpec(memory_space=pltpu.SMEM)
    params = pltpu.CompilerParams(vmem_limit_bytes=56 << 20)
    flat_width = columns + capacity + LANES
    piece_shape = jax.ShapeDtypeStruct((GROUP, part), F32)
    pieces_shape = jax.ShapeDtypeStruct((groups, levels_here, part), F32)
    group_shape = jax.ShapeDtypeStruct((groups, GROUP, part), F32)
    n_groups = levels_here // GROUP
    any_spec = pl.BlockSpec(memory_space=pl.ANY)

    def exchange(pieces):
        return lax.all_to_all(pieces, "lev", 0, 0, tiled=True)

    def permute(piece, turn):
        return lax.ppermute(piece, "lev", flip_pairs(groups, turn)) if turn else piece

    diffs, later, got = [], None, []
    for group in range(n_groups):
        before = [] if later is None else [later]
        n_sooner = groups if group else 1
        results = pl.pallas_call(
            functools.partial(forward_kernel, size_x, size_y, groups, n_sooner),
            grid=(1,),
            in_specs=[
                smem,
                pl.BlockSpec((1, GROUP, size_x, size_y), lambda g, group=group: (0, group, 0, 0)),
                pl.BlockSpec((GROUP, size_x, size_y), lambda g, group=group: (group, 0, 0)),
            ]
            + [any_spec] * len(before),
            out_specs=[
                pl.BlockSpec((size_x, GROUP, size_y), lambda g: (0, 0, 0)),
                pl.BlockSpec((groups, GROUP, part), lambda g, group=group: (0, group, 0)),
            ]
            + (
                [pl.BlockSpec((GROUP, part), lambda g: (0, 0))] * groups
                if group
                else [pl.BlockSpec((groups, GROUP, part), lambda g: (0, 0, 0))]
            ),
            out_shape=[jax.ShapeDtypeStruct((size_x, GROUP, size_y), F32), pieces_shape]
            + ([piece_shape] * groups if group else [group_shape]),
            input_output_aliases={3: 1} if before else {},
            scratch_shapes=[pltpu.VMEM((GROUP, flat_width), F32)]
            + [pltpu.VMEM((size_x, GROUP, size_y), F32)] * 5,
            compiler_params=params,
            cost_estimate=pl.CostEstimate(flops=0, bytes_accessed=0, transcendentals=0),
            name="smooth_and_cut",
        )(sub_widths, control, diffusivity, *before)
        diffs.append(results[0])
        later = results[1]
        if group:
            got += [permute(piece, turn) for piece, turn in zip(results[2:], turns_in(groups))]
        else:
            got.append(exchange(results[2]))

    width = sub_widths[me]
    live = jnp.arange(obs_cap, dtype=jnp.int32) < obs_counts[me]
    slots = jnp.where(live, obs_raw[0] % width, -1)[None, :]

    by_group = vertical_filter.reshape(levels, groups, n_groups, GROUP)
    def reordered(orders):
        places = [jnp.bitwise_xor(me, jnp.array(order, jnp.int32)) if order else jnp.arange(groups) for order in orders]
        return jnp.concatenate([by_group[:, at, g].reshape(levels, -1) for g, at in enumerate(places)], axis=1)

    last = n_groups - 1
    filter_in = reordered([turns_in(groups) if g else None for g in range(n_groups)])
    filter_out = reordered([turns_out(groups, g == last) for g in range(n_groups)])

    width = half
    blocks = part // width
    some = blocks // 2

    def block_of(g, core):
        return (g // some + core[0]) % 2 * some + g % some

    square = pl.BlockSpec((levels, levels), lambda g, core: (0, 0))
    slab = pl.BlockSpec((groups, levels_here, width), lambda g, core: (0, 0, block_of(g, core)))
    strip = pl.BlockSpec((GROUP, width), lambda g, core: (0, block_of(g, core)))
    group_slab = pl.BlockSpec((groups, GROUP, width), lambda g, core: (0, 0, block_of(g, core)))
    strips_in = [group_slab] + [strip] * (groups * (n_groups - 1))
    first_half = pl.BlockSpec((width, levels), lambda g, core: (jnp.minimum(g, some - 1), 0))
    second_half = pl.BlockSpec((width, levels), lambda g, core: (jnp.maximum(g - some, 0), 0))
    half_shape = jax.ShapeDtypeStruct((half, levels), F32)
    core = (lax.axis_index("mem") % 2).astype(jnp.int32)[None]
    table = pltpu.VMEM((2 * levels, 2 * levels), BF16)
    cost = pl.CostEstimate(flops=0, bytes_accessed=0, transcendentals=0)
    rows_here = 256

    def weights(c, slots):
        return pl.pallas_call(
            functools.partial(observation_kernel, part, c, obs_cap),
            grid=(half // rows_here,),
            in_specs=[
                pl.BlockSpec((1, obs_cap), lambda g: (0, 0)),
                pl.BlockSpec((1, obs_cap, levels), lambda g: (0, 0, 0)),
            ],
            out_specs=pl.BlockSpec((rows_here, levels), lambda g: (g, 0)),
            out_shape=jax.ShapeDtypeStruct((half, levels), F32),
            scratch_shapes=[pltpu.VMEM((obs_cap, 2 * levels), BF16)],
            compiler_params=params,
            cost_estimate=cost,
            name="observation_weights",
        )(slots, obs_rinv)

    def perturb_part(c):
        return pl.BlockSpec((1, width, levels), lambda g, core: (0, c * blocks + block_of(g, core), 0))

    def filter_forward(c, vfilter, *pieces):
        return pl.pallas_call(
            filter_kernel,
            grid_spec=pltpu.PrefetchScalarGridSpec(
                num_scalar_prefetch=1,
                grid=(blocks,),
                in_specs=[square, perturb_part(c)] + ([slab] if len(pieces) == 1 else strips_in),
                out_specs=[first_half, second_half],
                scratch_shapes=[table],
            ),
            out_shape=[half_shape, half_shape],
            compiler_params=params,
            cost_estimate=cost,
            name="filter_forward",
        )(core, vfilter, perturb, *pieces)

    def filter_backward(c, vfilter, adj_mine, adj_other, strips):
        return pl.pallas_call(
            functools.partial(back_kernel, len(adj_mine)),
            grid_spec=pltpu.PrefetchScalarGridSpec(
                num_scalar_prefetch=1,
                grid=(blocks,),
                in_specs=[square, perturb_part(c)]
                + [pl.BlockSpec(adj.shape, lambda g, core: (0, 0)) for adj in adj_mine + adj_other],
                out_specs=[strip] * (groups * n_groups) if strips else [slab],
                scratch_shapes=[table],
            ),
            out_shape=[piece_shape] * (groups * n_groups) if strips else [pieces_shape],
            compiler_params=params,
            cost_estimate=cost,
            name="filter_backward",
        )(core, vfilter, perturb, *adj_mine, *adj_other)

    def member_sum(keep, send, obs_weight, pieces):
        mine, other = [], []
        for first in range(0, half, half // pieces):
            here = slice(first, first + half // pieces)
            total = keep[here] + lax.ppermute(send[here], "mem", flip_pairs(n_mem, 1))
            bit = 2
            while bit < n_mem:
                total = total + lax.ppermute(total, "mem", flip_pairs(n_mem, bit))
                bit *= 2
            mine.append(total * obs_weight[here])
            other.append(lax.ppermute(mine[-1], "mem", flip_pairs(n_mem, 1)))
        return mine, other

    slots = after(slots, got[1], filter_out)
    weight = [weights(c, slots) for c in range(PARTS)]
    got_later = exchange(later)

    keep, send = filter_forward(0, filter_in, *got)
    mine, other = member_sum(keep, send, weight[0], 1)
    pieces = filter_backward(0, vertical_filter, mine, other, False)[0]
    back_sooner = exchange(pieces)

    keep, send = filter_forward(1, after(vertical_filter, pieces), got_later)
    mine, other = member_sum(keep, send, weight[1], 3)
    pieces = filter_backward(1, filter_out, mine, other, True)
    out = None
    for group in range(n_groups):
        before = [] if out is None else [out]
        back = []
        for piece, turn in zip(pieces[group * groups :], turns_out(groups, group == last)):
            back.append(permute(after(piece, out) if before and turn == 1 else piece, turn))
        out = pl.pallas_call(
            functools.partial(backward_kernel, size_x, size_y, groups, capacity, group, group == last),
            grid=(1,),
            in_specs=[smem, pl.BlockSpec((size_x, GROUP, size_y), lambda g: (0, 0, 0))]
            + [any_spec] * (1 + len(back) + len(before)),
            out_specs=pl.BlockSpec((1, GROUP, size_x, size_y), lambda g, group=group: (0, group, 0, 0)),
            out_shape=jax.ShapeDtypeStruct((members, levels_here, size_x, size_y), F32),
            input_output_aliases={3 + len(back): 0} if before else {},
            scratch_shapes=[
                pltpu.VMEM((groups, GROUP, capacity), F32),
                pltpu.VMEM((GROUP, flat_width), F32),
            ]
            + [pltpu.VMEM((size_x, GROUP, size_y), F32)] * 5
            + [pltpu.SemaphoreType.DMA((1 + groups,))],
            compiler_params=params,
            cost_estimate=pl.CostEstimate(flops=0, bytes_accessed=0, transcendentals=0),
            name="place_and_smooth",
        )(sub_widths, diffs[group], back_sooner, *back, *before)
    return out


def solution(mesh):
    return jax.shard_map(
        body,
        mesh=mesh,
        in_specs=(
            P("mem", "lev", None, None),
            P("lev", None, None),
            P("mem", "lev", None),
            P(),
            P(),
            P("lev", None),
            P(),
            P("lev", None, None),
        ),
        out_specs=P("mem", "lev", None, None),
        check_vma=False,
    )
```
